256 devices in a mesh: space: 16 (over z, x_hi), tm: 16 (over x_lo, y, core).
Axes of the slice: x: 4 (x_hi: 2, x_lo: 2; x = x_hi * 2 + x_lo), y: 4, z: 8, core: 2. Of those that a mesh axis runs over, the one named last changes fastest.
Arguments:
- snapshots: float32 [32768, 16384], P('space', 'tm'), may hold values from -3000 to 3000, as said below
- sketch: float32 [16384, 256], P('tm'), may hold values from -6 to 6
Outputs:
- refined: float32 [32768, 256], P('space')
- cosample: float32 [16384, 256], P('tm')
The draws below stay inside these ranges and needn't reach their ends.
Inputs may be any that keep to these rules, and one draw needn't show every extreme that they name: `snapshots`: float32 snapshot values.
All inputs are finite; a program needn't handle non-finite values.
Results may differ from the reference program's by a relative error of at most 0.000071.
Values sent between devices are 32-bit elements; how exact they have to be, the bound alone decides.
A program may use at most 64 MiB of HBM per device.

```python
import jax
import jax.numpy as jnp
from jax import lax

K = 256
POINTS = 32768
TIMES = 16384


def draw_snapshots(key, part):
    first, second, third = jax.random.split(key, 3)
    base = jnp.clip(jax.random.normal(first, (POINTS, TIMES), jnp.float32), -6.0, 6.0)
    cols = jnp.exp(jax.random.uniform(third, (1, TIMES), jnp.float32, 0.0, 2.3))
    rows = jnp.exp(jax.random.uniform(second, (POINTS, 1), jnp.float32, 0.0, 2.3))
    return base * rows * cols


def level_of(rng, extent, pieces, low, largest):
    gain, own = 1.0, jax.random.fold_in(rng, 6)
    for axis_at, shards_of in pieces:
        draws = jnp.exp(jax.random.uniform(jax.random.fold_in(own, axis_at), (shards_of,), jnp.float32, low / len(pieces), largest / len(pieces)))
        gain = gain * jnp.repeat(draws, extent[axis_at] // shards_of).reshape([-1 if axis == axis_at else 1 for axis in range(len(extent))])
    return gain


def gaussian(rng, extent, scale, limit, cuts=(), held_as=jnp.bfloat16):
    result = scale * jax.random.normal(rng, extent, jnp.float32)
    if cuts:
        result = result * level_of(rng, extent, cuts, -0.22, 0.18)
    return jnp.clip(result, -limit, limit).astype(held_as)


def setup_inputs(seed: int = 0) -> dict:
    seeds = jax.random.split(jax.random.key(seed), 3)
    return {
        "snapshots": draw_snapshots(jax.random.fold_in(seeds[2], 71), 0),
        "sketch": gaussian(seeds[1], (TIMES, K), 1.0, 6.0, ((0, 16),), jnp.float32),
    }


EPS = 1e-06

def scale_rows(value):
    return value * lax.rsqrt(lax.optimization_barrier(jnp.mean(value * value, axis=1, keepdims=True)) + EPS)

def reference(snapshots, sketch):
    sample = scale_rows(jnp.dot(snapshots, sketch, precision=lax.Precision.HIGHEST, preferred_element_type=jnp.float32))
    cosample = scale_rows(lax.dot_general(snapshots, sample, (((0,), (0,)), ((), ())), precision=lax.Precision.HIGHEST, preferred_element_type=jnp.float32))
    refined = scale_rows(jnp.dot(snapshots, cosample, precision=lax.Precision.HIGHEST, preferred_element_type=jnp.float32))
    return (refined, cosample)
```

```python
import functools

import jax
import jax.numpy as jnp
from jax import lax
from jax.experimental import pallas as pl
from jax.experimental.pallas import tpu as pltpu
from jax.sharding import PartitionSpec as P

EPS = 1e-06
MESH = pl.DeviceIdType.MESH
F32, BF16 = jnp.float32, jnp.bfloat16
NZ, NY = 8, 4
N = 4
NB = 4


def split(value):
    high = value.astype(BF16)
    return high, (value - high.astype(F32)).astype(BF16)


def scale_rows(value):
    return value * lax.rsqrt(jnp.mean(value * value, axis=1, keepdims=True) + EPS)


def dot(a, b):
    return jnp.dot(a, b, preferred_element_type=F32)


def dot_t(a, b):
    return lax.dot_general(a, b, (((0,), (0,)), ((), ())), preferred_element_type=F32)


def kernel(
    snap_ref, sketch_ref, refined_ref, cosample_ref,
    wide, s_hi, s_lo, b_hi, b_lo, part, sample, p_hi, p_lo, back, c_hi, c_lo, last,
    from_core, from_y, from_x, from_x2, from_y2, from_xh, from_z,
    load_sem, send_sem, recv_sem, send_sem_b, recv_sem_b,
):
    points, times = wide.shape
    space, tm = lax.axis_index("space"), lax.axis_index("tm")
    z, xh = space // 2, lax.rem(space, 2)
    xl, y, core = tm // 8, lax.rem(tm // 2, 4), lax.rem(tm, 2)

    def at_tm(xl, y, core):
        return {"space": space, "tm": xl * 8 + y * 2 + core}

    def at_space(z, xh):
        return {"space": z * 2 + xh, "tm": tm}

    other_core, other_x = at_tm(xl, y, 1 - core), at_tm(1 - xl, y, core)
    other_xh = at_space(z, 1 - xh)
    y_at = [lax.rem(y + d, NY) for d in range(NY)]
    z_at = [lax.rem(z + d, NZ) for d in range(NZ)]
    peer_y = [at_tm(xl, y_at[d], core) for d in range(NY)]
    peer_z = [at_space(z_at[d], xh) for d in range(NZ)]

    chunk = points // N
    width = times // NB

    def load(i):
        rows = pl.ds(pl.multiple_of(i * chunk, chunk), chunk)
        return pltpu.make_async_copy(snap_ref.at[rows], wide.at[rows], load_sem.at[i])

    for i in range(N):
        load(i).start()

    barrier = pltpu.get_barrier_semaphore()
    peers = [other_core, other_x, other_xh, *peer_y[1:], *peer_z[1:]]
    for peer in peers:
        pl.semaphore_signal(barrier, inc=1, device_id=peer, device_id_type=MESH)

    b_hi[...], b_lo[...] = split(sketch_ref[...])
    back[...] = jnp.zeros_like(back)
    last[...] = jnp.zeros_like(last)
    pl.semaphore_wait(barrier, len(peers))

    def send(src, dst, sent, arrived, peer):
        pltpu.make_async_remote_copy(
            src_ref=src, dst_ref=dst, send_sem=sent, recv_sem=arrived, device_id=peer, device_id_type=MESH
        ).start()

    def take(rows, sem):
        ref = part.at[pl.ds(0, rows)]
        pltpu.make_async_copy(ref, ref, sem).wait()

    def rows_of(start, size):
        return pl.ds(pl.multiple_of(start, 8), size)

    half = chunk // 2
    sub = half // 2

    def tm_stages(phase, multiply, summed, gathered):
        sent, got = send_sem.at[phase], recv_sem.at[phase]

        def mine(i):
            return i * chunk + core * half

        def first(i):
            multiply(i)
            src = rows_of(i * chunk + (1 - core) * half, half)
            send(summed.at[src], from_core.at[phase, i], sent.at[0], got.at[0, i], other_core)

        def over_1(i):
            take(half, got.at[0, i])
            a, b = mine(i), mine(i) + sub
            own = rows_of(a, half)
            summed[own, :] += from_core[phase, i]
            for d in (2, 1, 3):
                src = rows_of(a + y_at[d] * (sub // 4), sub // 4)
                send(summed.at[src], from_y.at[phase, i, d - 1], sent.at[1], got.at[1, i], peer_y[d])
            src = rows_of(b + (1 - xl) * (sub // 2), sub // 2)
            send(summed.at[src], from_x.at[phase, i], sent.at[1], got.at[1, i], other_x)

        def over_2(i):
            take(3 * (sub // 4) + sub // 2, got.at[1, i])
            a, b = mine(i) + y * (sub // 4), mine(i) + sub + xl * (sub // 2)
            own = rows_of(a, sub // 4)
            summed[own, :] += from_y[phase, i, 0] + from_y[phase, i, 1] + from_y[phase, i, 2]
            own = rows_of(b, sub // 2)
            summed[own, :] += from_x[phase, i]
            for d in (2, 1, 3):
                src = rows_of(b + y_at[d] * (sub // 8), sub // 8)
                send(summed.at[src], from_y2.at[phase, i, d - 1], sent.at[2], got.at[2, i], peer_y[d])
            src = rows_of(a + (1 - xl) * (sub // 8), sub // 8)
            send(summed.at[src], from_x2.at[phase, i], sent.at[2], got.at[2, i], other_x)

        def finish(i):
            take(4 * (sub // 8), got.at[2, i])
            a = rows_of(mine(i) + y * (sub // 4) + xl * (sub // 8), sub // 8)
            b = rows_of(mine(i) + sub + xl * (sub // 2) + y * (sub // 8), sub // 8)
            total = summed[b, :] + (from_y2[phase, i, 0] + from_y2[phase, i, 1] + from_y2[phase, i, 2])
            gathered[b, :] = scale_rows(total)
            for d in (2, 1, 3):
                send(gathered.at[b], gathered.at[b], sent.at[3], got.at[3, i], peer_y[d])
            gathered[a, :] = scale_rows(summed[a, :] + from_x2[phase, i])
            send(gathered.at[a], gathered.at[a], sent.at[3], got.at[3, i], other_x)

        def spread(i):
            take(4 * (sub // 8), got.at[3, i])
            a = rows_of(mine(i) + y * (sub // 4), sub // 4)
            b = rows_of(mine(i) + sub + xl * (sub // 2), sub // 2)
            for d in (2, 1, 3):
                send(gathered.at[a], gathered.at[a], sent.at[4], got.at[4, i], peer_y[d])
            send(gathered.at[b], gathered.at[b], sent.at[4], got.at[4, i], other_x)

        def to_core(i):
            take(3 * (sub // 4) + sub // 2, got.at[4, i])
            own = rows_of(mine(i), half)
            send(gathered.at[own], gathered.at[own], sent.at[5], got.at[5, i], other_core)

        def arrive(i):
            take(half, got.at[5, i])

        def close():
            for stage, rows in enumerate((half, 5 * (sub // 4), sub // 2, sub // 2, 5 * (sub // 4), half)):
                take(N * rows, sent.at[stage])

        return [first, over_1, over_2, finish, spread, to_core], arrive, close

    def space_stages(multiply):
        half = width // 2
        piece = half // NZ

        def first(j):
            multiply(j)
            src = rows_of(j * width + (1 - xh) * half, half)
            send(back.at[src], from_xh.at[j], send_sem_b.at[0], recv_sem_b.at[0, j], other_xh)

        def over(j):
            take(half, recv_sem_b.at[0, j])
            a = j * width + xh * half
            own = rows_of(a, half)
            back[own, :] += from_xh[j]
            for d in (4, 3, 5, 2, 6, 1, 7):
                src = rows_of(a + z_at[d] * piece, piece)
                send(back.at[src], from_z.at[j, d - 1], send_sem_b.at[1], recv_sem_b.at[1, j], peer_z[d])

        def finish(j):
            take(7 * piece, recv_sem_b.at[1, j])
            own = rows_of(j * width + xh * half + z * piece, piece)
            total = back[own, :]
            for d in range(1, NZ):
                total += from_z[j, d - 1]
            cosample_ref[own, :] = scale_rows(total)
            for d in (4, 3, 5, 2, 6, 1, 7):
                send(cosample_ref.at[own], cosample_ref.at[own], send_sem_b.at[2], recv_sem_b.at[2, j], peer_z[d])

        def spread(j):
            take(7 * piece, recv_sem_b.at[2, j])
            own = rows_of(j * width + xh * half, half)
            send(cosample_ref.at[own], cosample_ref.at[own], send_sem_b.at[3], recv_sem_b.at[3, j], other_xh)

        def arrive(j):
            take(half, recv_sem_b.at[3, j])

        def close():
            for stage, rows in enumerate((half, 7 * piece, 7 * piece, half)):
                take(NB * rows, send_sem_b.at[stage])

        return [first, over, finish, spread], arrive, close

    def run(stages, parts, steps):
        def step(t, _):
            for s in reversed(range(len(stages))):
                stage, count = stages[s], parts[s]

                @pl.when((t >= s) & (t < s + count))
                def _():
                    stage(t - s)

            return 0

        lax.fori_loop(0, steps, step, 0)

    def multiply_1(i):
        load(i).wait()

        def piece(q, _):
            rows = pl.ds(pl.multiple_of(i * chunk + q * 256, 256), 256)
            high, low = split(wide[rows, :])
            s_hi[rows, :] = high
            s_lo[rows, :] = low
            part[rows, :] = dot(high, b_hi[...]) + (dot(high, b_lo[...]) + dot(low, b_hi[...]))
            return 0

        lax.fori_loop(0, chunk // 256, piece, 0)

    def add_back(i, j):
        rows = pl.ds(pl.multiple_of(i * chunk, chunk), chunk)
        columns = pl.ds(pl.multiple_of(j * width, width), width)
        high, low = s_hi[rows, columns], s_lo[rows, columns]
        back[columns, :] += dot_t(high, p_hi[...]) + (dot_t(high, p_lo[...]) + dot_t(low, p_hi[...]))

    def split_sample(i):
        rows = pl.ds(pl.multiple_of(i * chunk, chunk), chunk)
        p_hi[...], p_lo[...] = split(sample[rows, :])

    stages, arrive_1, close_1 = tm_stages(0, multiply_1, part, sample)

    def use_sample(i):
        arrive_1(i)
        split_sample(i)
        lax.fori_loop(0, NB, lambda j, _: (add_back(i, j), 0)[1], 0)

    run([*stages, use_sample], [N] * 6 + [N - 1], N + 5)
    arrive_1(N - 1)
    split_sample(N - 1)

    def add_last(i, j):
        rows = pl.ds(pl.multiple_of(i * chunk, chunk), chunk)
        columns = pl.ds(pl.multiple_of(j * width, width), width)
        high, low = s_hi[rows, columns], s_lo[rows, columns]
        last[rows, :] += dot(high, c_hi[...]) + (dot(high, c_lo[...]) + dot(low, c_hi[...]))

    def split_cosample(j):
        rows = pl.ds(pl.multiple_of(j * width, width), width)
        c_hi[...], c_lo[...] = split(cosample_ref[rows, :])

    stages, arrive_b, close_b = space_stages(functools.partial(add_back, N - 1))

    def use_cosample(j):
        arrive_b(j)
        split_cosample(j)
        lax.fori_loop(0, N, lambda i, _: (add_last(i, j), 0)[1], 0)

    run([*stages, use_cosample], [NB] * 4 + [NB - 1], NB + 3)
    arrive_b(NB - 1)
    split_cosample(NB - 1)

    stages, arrive_2, close_2 = tm_stages(1, lambda i: add_last(i, NB - 1), last, refined_ref)
    run([*stages, arrive_2], [N] * 7, N + 6)
    close_1()
    close_b()
    close_2()


def local(snapshots, sketch):
    (points, times), k = snapshots.shape, sketch.shape[1]
    chunk, width = points // N, times // NB
    half = chunk // 2
    sub = half // 2
    vmem = pl.BlockSpec(memory_space=pltpu.VMEM)
    return pl.pallas_call(
        kernel,
        name="window",
        out_shape=[jax.ShapeDtypeStruct((points, k), F32), jax.ShapeDtypeStruct((times, k), F32)],
        in_specs=[pl.BlockSpec(memory_space=pl.ANY), vmem],
        out_specs=[vmem, vmem],
        scratch_shapes=[
            pltpu.VMEM((points, times), F32),
            pltpu.VMEM((points, times), BF16),
            pltpu.VMEM((points, times), BF16),
            pltpu.VMEM((times, k), BF16),
            pltpu.VMEM((times, k), BF16),
            pltpu.VMEM((points, k), F32),
            pltpu.VMEM((points, k), F32),
            pltpu.VMEM((chunk, k), BF16),
            pltpu.VMEM((chunk, k), BF16),
            pltpu.VMEM((times, k), F32),
            pltpu.VMEM((width, k), BF16),
            pltpu.VMEM((width, k), BF16),
            pltpu.VMEM((points, k), F32),
            pltpu.VMEM((2, N, half, k), F32),
            pltpu.VMEM((2, N, 3, sub // 4, k), F32),
            pltpu.VMEM((2, N, sub // 2, k), F32),
            pltpu.VMEM((2, N, sub // 8, k), F32),
            pltpu.VMEM((2, N, 3, sub // 8, k), F32),
            pltpu.VMEM((NB, width // 2, k), F32),
            pltpu.VMEM((NB, NZ - 1, width // 2 // NZ, k), F32),
            pltpu.SemaphoreType.DMA((N,)),
            pltpu.SemaphoreType.DMA((2, 6)),
            pltpu.SemaphoreType.DMA((2, 6, N)),
            pltpu.SemaphoreType.DMA((4,)),
            pltpu.SemaphoreType.DMA((4, NB)),
        ],
        compiler_params=pltpu.CompilerParams(
            collective_id=0, has_side_effects=True, vmem_limit_bytes=52 << 20
        ),
        cost_estimate=pl.CostEstimate(
            flops=18 * points * times * k, bytes_accessed=4 * points * times, transcendentals=0
        ),
    )(snapshots, sketch)


def solution(mesh):
    return jax.shard_map(
        local,
        mesh=mesh,
        in_specs=(P("space", "tm"), P("tm", None)),
        out_specs=(P("space", None), P("tm", None)),
        check_vma=False,
    )
```

```python
import functools

import jax
import jax.numpy as jnp
from jax import lax
from jax.experimental import pallas as pl
from jax.experimental.pallas import tpu as pltpu
from jax.sharding import PartitionSpec as P

EPS = 1e-06
MESH = pl.DeviceIdType.MESH
F32, BF16 = jnp.float32, jnp.bfloat16
NZ, NY = 8, 4
N = 4
NB = 4
ORDER_1 = [
    (0, 0), (0, 1), (1, 0), (0, 2), (1, 1), (0, 3), (2, 0), (1, 2), (1, 3), (2, 1), (3, 0), (2, 2), (2, 3), (3, 1),
    (4, 0), (3, 2), (3, 3), (4, 1), (5, 0), (4, 2), (4, 3), (6, 0), (5, 1), (6, 1), (5, 2), (5, 3), (6, 2),
]
ORDER_B = [
    (0, 0), (0, 1), (0, 2), (0, 3), (1, 0), (1, 1), (1, 2), (2, 0), (1, 3), (2, 1), (2, 2), (3, 0), (2, 3), (3, 1),
    (4, 0), (3, 2), (3, 3), (4, 1), (4, 2),
]
ORDER_2 = [(stage, i) for stage in range(5) for i in range(N)] + [
    (5, 0), (5, 1), (6, 0), (5, 2), (6, 1), (5, 3), (6, 2), (6, 3),
]


def split(value):
    high = value.astype(BF16)
    return high, (value - high.astype(F32)).astype(BF16)


def scale_rows(value):
    return value * lax.rsqrt(jnp.mean(value * value, axis=1, keepdims=True) + EPS)


def dot(a, b):
    return jnp.dot(a, b, preferred_element_type=F32)


def dot_t(a, b):
    return lax.dot_general(a, b, (((0,), (0,)), ((), ())), preferred_element_type=F32)


def kernel(
    snap_ref, sketch_ref, refined_ref, cosample_ref,
    wide, s_hi, s_lo, b_hi, b_lo, part, sample, p_hi, p_lo, back, c_hi, c_lo, last,
    from_core, from_y, from_x, from_x2, from_y2, from_xh, from_z,
    load_sem, send_sem, recv_sem, send_sem_b, recv_sem_b,
):
    points, times = wide.shape
    space, tm = lax.axis_index("space"), lax.axis_index("tm")
    z, xh = space // 2, lax.rem(space, 2)
    xl, y, core = tm // 8, lax.rem(tm // 2, 4), lax.rem(tm, 2)

    def at_tm(xl, y, core):
        return {"space": space, "tm": xl * 8 + y * 2 + core}

    def at_space(z, xh):
        return {"space": z * 2 + xh, "tm": tm}

    other_core, other_x = at_tm(xl, y, 1 - core), at_tm(1 - xl, y, core)
    other_xh = at_space(z, 1 - xh)
    y_at = [lax.rem(y + d, NY) for d in range(NY)]
    z_at = [lax.rem(z + d, NZ) for d in range(NZ)]
    peer_y = [at_tm(xl, y_at[d], core) for d in range(NY)]
    peer_z = [at_space(z_at[d], xh) for d in range(NZ)]

    chunk = points // N
    width = times // NB

    def load(i):
        rows = pl.ds(pl.multiple_of(i * chunk, chunk), chunk)
        return pltpu.make_async_copy(snap_ref.at[rows], wide.at[rows], load_sem.at[i])

    for i in range(N):
        load(i).start()

    barrier = pltpu.get_barrier_semaphore()
    peers = [other_core, other_x, other_xh, *peer_y[1:], *peer_z[1:]]
    for peer in peers:
        pl.semaphore_signal(barrier, inc=1, device_id=peer, device_id_type=MESH)

    b_hi[...], b_lo[...] = split(sketch_ref[...])
    back[...] = jnp.zeros_like(back)
    last[...] = jnp.zeros_like(last)
    pl.semaphore_wait(barrier, len(peers))

    def send(src, dst, sent, arrived, peer):
        pltpu.make_async_remote_copy(
            src_ref=src, dst_ref=dst, send_sem=sent, recv_sem=arrived, device_id=peer, device_id_type=MESH
        ).start()

    def take(rows, sem):
        ref = part.at[pl.ds(0, rows)]
        pltpu.make_async_copy(ref, ref, sem).wait()

    def rows_of(start, size):
        return pl.ds(pl.multiple_of(start, 8), size)

    half = chunk // 2
    sub = half // 2

    def tm_stages(phase, multiply, summed, gathered):
        sent, got = send_sem.at[phase], recv_sem.at[phase]

        def mine(i):
            return i * chunk + core * half

        def first(i):
            multiply(i)
            src = rows_of(i * chunk + (1 - core) * half, half)
            send(summed.at[src], from_core.at[phase, i], sent.at[0], got.at[0, i], other_core)

        def over_1(i):
            take(half, got.at[0, i])
            a, b = mine(i), mine(i) + sub
            own = rows_of(a, half)
            summed[own, :] += from_core[phase, i]
            for d in (2, 1, 3):
                src = rows_of(a + y_at[d] * (sub // 4), sub // 4)
                send(summed.at[src], from_y.at[phase, i, d - 1], sent.at[1], got.at[1, i], peer_y[d])
            src = rows_of(b + (1 - xl) * (sub // 2), sub // 2)
            send(summed.at[src], from_x.at[phase, i], sent.at[1], got.at[1, i], other_x)

        def over_2(i):
            take(3 * (sub // 4) + sub // 2, got.at[1, i])
            a, b = mine(i) + y * (sub // 4), mine(i) + sub + xl * (sub // 2)
            own = rows_of(a, sub // 4)
            summed[own, :] += from_y[phase, i, 0] + from_y[phase, i, 1] + from_y[phase, i, 2]
            own = rows_of(b, sub // 2)
            summed[own, :] += from_x[phase, i]
            for d in (2, 1, 3):
                src = rows_of(b + y_at[d] * (sub // 8), sub // 8)
                send(summed.at[src], from_y2.at[phase, i, d - 1], sent.at[2], got.at[2, i], peer_y[d])
            src = rows_of(a + (1 - xl) * (sub // 8), sub // 8)
            send(summed.at[src], from_x2.at[phase, i], sent.at[2], got.at[2, i], other_x)

        def finish(i):
            take(4 * (sub // 8), got.at[2, i])
            a = rows_of(mine(i) + y * (sub // 4) + xl * (sub // 8), sub // 8)
            b = rows_of(mine(i) + sub + xl * (sub // 2) + y * (sub // 8), sub // 8)
            total = summed[b, :] + (from_y2[phase, i, 0] + from_y2[phase, i, 1] + from_y2[phase, i, 2])
            gathered[b, :] = scale_rows(total)
            for d in (2, 1, 3):
                send(gathered.at[b], gathered.at[b], sent.at[3], got.at[3, i], peer_y[d])
            gathered[a, :] = scale_rows(summed[a, :] + from_x2[phase, i])
            send(gathered.at[a], gathered.at[a], sent.at[3], got.at[3, i], other_x)

        def spread(i):
            take(4 * (sub // 8), got.at[3, i])
            a = rows_of(mine(i) + y * (sub // 4), sub // 4)
            b = rows_of(mine(i) + sub + xl * (sub // 2), sub // 2)
            for d in (2, 1, 3):
                send(gathered.at[a], gathered.at[a], sent.at[4], got.at[4, i], peer_y[d])
            send(gathered.at[b], gathered.at[b], sent.at[4], got.at[4, i], other_x)

        def to_core(i):
            take(3 * (sub // 4) + sub // 2, got.at[4, i])
            own = rows_of(mine(i), half)
            send(gathered.at[own], gathered.at[own], sent.at[5], got.at[5, i], other_core)

        def arrive(i):
            take(half, got.at[5, i])

        def close():
            for stage, rows in enumerate((half, 5 * (sub // 4), sub // 2, sub // 2, 5 * (sub // 4), half)):
                take(N * rows, sent.at[stage])

        return [first, over_1, over_2, finish, spread, to_core], arrive, close

    def space_stages(multiply):
        half = width // 2
        piece = half // NZ

        def first(j):
            multiply(j)
            src = rows_of(j * width + (1 - xh) * half, half)
            send(back.at[src], from_xh.at[j], send_sem_b.at[0], recv_sem_b.at[0, j], other_xh)

        def over(j):
            take(half, recv_sem_b.at[0, j])
            a = j * width + xh * half
            own = rows_of(a, half)
            back[own, :] += from_xh[j]
            for d in (4, 3, 5, 2, 6, 1, 7):
                src = rows_of(a + z_at[d] * piece, piece)
                send(back.at[src], from_z.at[j, d - 1], send_sem_b.at[1], recv_sem_b.at[1, j], peer_z[d])

        def finish(j):
            take(7 * piece, recv_sem_b.at[1, j])
            own = rows_of(j * width + xh * half + z * piece, piece)
            total = back[own, :]
            for d in range(1, NZ):
                total += from_z[j, d - 1]
            cosample_ref[own, :] = scale_rows(total)
            for d in (4, 3, 5, 2, 6, 1, 7):
                send(cosample_ref.at[own], cosample_ref.at[own], send_sem_b.at[2], recv_sem_b.at[2, j], peer_z[d])

        def spread(j):
            take(7 * piece, recv_sem_b.at[2, j])
            own = rows_of(j * width + xh * half, half)
            send(cosample_ref.at[own], cosample_ref.at[own], send_sem_b.at[3], recv_sem_b.at[3, j], other_xh)

        def arrive(j):
            take(half, recv_sem_b.at[3, j])

        def close():
            for stage, rows in enumerate((half, 7 * piece, 7 * piece, half)):
                take(NB * rows, send_sem_b.at[stage])

        return [first, over, finish, spread], arrive, close

    def run(stages, order):
        for stage, part_at in order:
            stages[stage](part_at)

    def multiply_1(i):
        load(i).wait()

        def piece(q, _):
            rows = pl.ds(pl.multiple_of(i * chunk + q * 256, 256), 256)
            high, low = split(wide[rows, :])
            s_hi[rows, :] = high
            s_lo[rows, :] = low
            part[rows, :] = dot(high, b_hi[...]) + (dot(high, b_lo[...]) + dot(low, b_hi[...]))
            return 0

        lax.fori_loop(0, chunk // 256, piece, 0)

    def add_back(i, j):
        rows = pl.ds(pl.multiple_of(i * chunk, chunk), chunk)
        columns = pl.ds(pl.multiple_of(j * width, width), width)
        high, low = s_hi[rows, columns], s_lo[rows, columns]
        back[columns, :] += dot_t(high, p_hi[...]) + (dot_t(high, p_lo[...]) + dot_t(low, p_hi[...]))

    def split_sample(i):
        rows = pl.ds(pl.multiple_of(i * chunk, chunk), chunk)
        p_hi[...], p_lo[...] = split(sample[rows, :])

    stages, arrive_1, close_1 = tm_stages(0, multiply_1, part, sample)

    def use_sample(i):
        arrive_1(i)
        split_sample(i)
        lax.fori_loop(0, NB, lambda j, _: (add_back(i, j), 0)[1], 0)

    run([*stages, use_sample], ORDER_1)
    arrive_1(N - 1)
    split_sample(N - 1)

    def add_last(i, j):
        rows = pl.ds(pl.multiple_of(i * chunk, chunk), chunk)
        columns = pl.ds(pl.multiple_of(j * width, width), width)
        high, low = s_hi[rows, columns], s_lo[rows, columns]
        last[rows, :] += dot(high, c_hi[...]) + (dot(high, c_lo[...]) + dot(low, c_hi[...]))

    def split_cosample(j):
        rows = pl.ds(pl.multiple_of(j * width, width), width)
        c_hi[...], c_lo[...] = split(cosample_ref[rows, :])

    stages, arrive_b, close_b = space_stages(functools.partial(add_back, N - 1))

    def use_cosample(j):
        arrive_b(j)
        split_cosample(j)
        lax.fori_loop(0, N, lambda i, _: (add_last(i, j), 0)[1], 0)

    run([*stages, use_cosample], ORDER_B)
    arrive_b(NB - 1)
    split_cosample(NB - 1)

    stages, arrive_2, close_2 = tm_stages(1, lambda i: add_last(i, NB - 1), last, refined_ref)
    run([*stages, arrive_2], ORDER_2)
    close_1()
    close_b()
    close_2()


def local(snapshots, sketch):
    (points, times), k = snapshots.shape, sketch.shape[1]
    chunk, width = points // N, times // NB
    half = chunk // 2
    sub = half // 2
    vmem = pl.BlockSpec(memory_space=pltpu.VMEM)
    return pl.pallas_call(
        kernel,
        name="window",
        out_shape=[jax.ShapeDtypeStruct((points, k), F32), jax.ShapeDtypeStruct((times, k), F32)],
        in_specs=[pl.BlockSpec(memory_space=pltpu.HBM), vmem],
        out_specs=[vmem, vmem],
        scratch_shapes=[
            pltpu.VMEM((points, times), F32),
            pltpu.VMEM((points, times), BF16),
            pltpu.VMEM((points, times), BF16),
            pltpu.VMEM((times, k), BF16),
            pltpu.VMEM((times, k), BF16),
            pltpu.VMEM((points, k), F32),
            pltpu.VMEM((points, k), F32),
            pltpu.VMEM((chunk, k), BF16),
            pltpu.VMEM((chunk, k), BF16),
            pltpu.VMEM((times, k), F32),
            pltpu.VMEM((width, k), BF16),
            pltpu.VMEM((width, k), BF16),
            pltpu.VMEM((points, k), F32),
            pltpu.VMEM((2, N, half, k), F32),
            pltpu.VMEM((2, N, 3, sub // 4, k), F32),
            pltpu.VMEM((2, N, sub // 2, k), F32),
            pltpu.VMEM((2, N, sub // 8, k), F32),
            pltpu.VMEM((2, N, 3, sub // 8, k), F32),
            pltpu.VMEM((NB, width // 2, k), F32),
            pltpu.VMEM((NB, NZ - 1, width // 2 // NZ, k), F32),
            pltpu.SemaphoreType.DMA((N,)),
            pltpu.SemaphoreType.DMA((2, 6)),
            pltpu.SemaphoreType.DMA((2, 6, N)),
            pltpu.SemaphoreType.DMA((4,)),
            pltpu.SemaphoreType.DMA((4, NB)),
        ],
        compiler_params=pltpu.CompilerParams(
            collective_id=0, has_side_effects=True, vmem_limit_bytes=40 << 20
        ),
        cost_estimate=pl.CostEstimate(
            flops=18 * points * times * k, bytes_accessed=4 * points * times, transcendentals=0
        ),
    )(snapshots, sketch)


def solution(mesh):
    return jax.shard_map(
        local,
        mesh=mesh,
        in_specs=(P("space", "tm"), P("tm", None)),
        out_specs=(P("space", None), P("tm", None)),
        check_vma=False,
    )
```

```python
import jax
import jax.numpy as jnp
from jax import lax
from jax.experimental import pallas as pl
from jax.experimental.pallas import tpu as pltpu
from jax.sharding import PartitionSpec as P

EPS = 1e-06
MESH = pl.DeviceIdType.MESH
F32, BF16 = jnp.float32, jnp.bfloat16
NZ, NY = 8, 4
H = 128
N = 4
NB = 4
ORDER = [
    (0, 0, 0, 0), (0, 0, 1, 0), (0, 1, 0, 0), (0, 0, 2, 0), (0, 1, 1, 0), (0, 0, 3, 0), (0, 2, 0, 0), (0, 1, 2, 0),
    (0, 1, 3, 0), (0, 2, 1, 0), (0, 3, 0, 0), (0, 2, 2, 0), (0, 2, 3, 0), (0, 3, 1, 0), (0, 4, 0, 0), (0, 3, 2, 0),
    (0, 3, 3, 0), (0, 3, 0, 1), (0, 3, 1, 1), (0, 4, 1, 0), (0, 3, 2, 1), (0, 3, 3, 1), (0, 5, 0, 0), (0, 4, 2, 0),
    (0, 6, 0, 0), (0, 4, 3, 0), (0, 4, 0, 1), (0, 4, 1, 1), (0, 5, 1, 0), (0, 4, 2, 1), (0, 4, 3, 1), (0, 6, 1, 0),
    (0, 5, 2, 0), (0, 5, 3, 0), (0, 5, 0, 1), (0, 6, 2, 0), (0, 6, 3, 0), (0, 5, 1, 1), (0, 5, 2, 1), (1, 0, 0, 0),
    (1, 0, 1, 0), (0, 5, 3, 1), (1, 0, 2, 0), (1, 0, 3, 0), (0, 6, 0, 1), (0, 6, 1, 1), (0, 6, 2, 1), (0, 6, 3, 1),
    (1, 1, 0, 0), (1, 0, 0, 1), (1, 0, 1, 1), (1, 0, 2, 1), (1, 0, 3, 1), (1, 1, 1, 0), (1, 1, 2, 0), (1, 1, 3, 0),
    (1, 1, 0, 1), (1, 1, 1, 1), (1, 1, 2, 1), (1, 1, 3, 1), (1, 2, 0, 0), (1, 2, 1, 0), (1, 2, 2, 0), (1, 2, 3, 0),
    (1, 2, 0, 1), (1, 2, 1, 1), (1, 2, 2, 1), (1, 2, 3, 1), (1, 3, 0, 0), (1, 3, 1, 0), (1, 3, 2, 0), (1, 4, 0, 0),
    (1, 3, 3, 0), (1, 4, 1, 0), (1, 3, 0, 1), (1, 4, 2, 0), (1, 3, 1, 1), (1, 3, 2, 1), (1, 4, 3, 0), (2, 0, 0, 0),
    (2, 0, 1, 0), (2, 0, 2, 0), (2, 0, 3, 0), (1, 3, 3, 1), (1, 4, 0, 1), (2, 1, 0, 0), (2, 1, 1, 0), (2, 1, 2, 0),
    (2, 1, 3, 0), (1, 4, 1, 1), (1, 4, 2, 1), (1, 4, 3, 1), (2, 2, 0, 0), (2, 0, 0, 1), (2, 0, 1, 1), (2, 2, 1, 0),
    (2, 0, 2, 1), (2, 0, 3, 1), (2, 2, 2, 0), (2, 1, 0, 1), (2, 1, 1, 1), (2, 2, 3, 0), (2, 1, 2, 1), (2, 1, 3, 1),
    (2, 2, 0, 1), (2, 2, 1, 1), (2, 2, 2, 1), (2, 2, 3, 1), (2, 3, 0, 0), (2, 3, 1, 0), (2, 3, 2, 0), (2, 3, 3, 0),
    (2, 4, 0, 0), (2, 4, 1, 0), (2, 4, 2, 0), (2, 4, 3, 0), (2, 5, 0, 0), (2, 5, 1, 0), (2, 6, 0, 0), (2, 5, 2, 0),
    (2, 6, 1, 0), (2, 5, 3, 0), (2, 6, 2, 0), (2, 6, 3, 0),
]


def split(value):
    high = value.astype(BF16)
    return high, (value - high.astype(F32)).astype(BF16)


def scale_halves(left, right):
    squares = jnp.sum(left * left + right * right, axis=1, keepdims=True)
    factor = lax.rsqrt(squares * (1.0 / (2 * H)) + EPS)
    return left * factor, right * factor


def dot(a, b):
    return jnp.dot(a, b, preferred_element_type=F32)


def dot_t(a, b):
    return lax.dot_general(a, b, (((0,), (0,)), ((), ())), preferred_element_type=F32)


def kernel(
    snap_ref, sketch_ref, refined_ref, cosample_ref,
    wide, s_hi, s_lo, b_hi, b_lo, part, sample, p_terms, back, cosample, c_terms, last,
    core_1, y_1, x_1, x2_1, y2_1, core_2, y_2, x_2, x2_2, y2_2, from_xh, from_z,
    load_sem, sent, sum_1, gather_1, got_b, sum_2, gather_2,
):
    points, times = wide.shape
    space, tm = lax.axis_index("space"), lax.axis_index("tm")
    z, xh = space // 2, lax.rem(space, 2)
    xl, y, core = tm // 8, lax.rem(tm // 2, 4), lax.rem(tm, 2)

    def at_tm(xl, y, core):
        return {"space": space, "tm": xl * 8 + y * 2 + core}

    def at_space(z, xh):
        return {"space": z * 2 + xh, "tm": tm}

    other_core, other_x = at_tm(xl, y, 1 - core), at_tm(1 - xl, y, core)
    other_xh = at_space(z, 1 - xh)
    y_at = [lax.rem(y + d, NY) for d in range(NY)]
    z_at = [lax.rem(z + d, NZ) for d in range(NZ)]
    peer_y = [at_tm(xl, y_at[d], core) for d in range(NY)]
    peer_z = [at_space(z_at[d], xh) for d in range(NZ)]
    y_order, z_order = (2, 1, 3), (4, 3, 5, 2, 6, 1, 7)

    chunk, width = points // N, times // NB
    half, sub = chunk // 2, chunk // 4
    half_b = width // 2
    piece = half_b // NZ

    def load(i):
        rows = pl.ds(pl.multiple_of(i * chunk, chunk), chunk)
        return pltpu.make_async_copy(snap_ref.at[rows], wide.at[rows], load_sem.at[i])

    for i in range(N):
        load(i).start()

    barrier = pltpu.get_barrier_semaphore()
    peers = [other_core, other_x, other_xh, *peer_y[1:], *peer_z[1:]]
    for peer in peers:
        pl.semaphore_signal(barrier, inc=1, device_id=peer, device_id_type=MESH)

    b_hi[...], b_lo[...] = split(sketch_ref[...])
    back[...] = jnp.zeros_like(back)
    last[...] = jnp.zeros_like(last)
    pl.semaphore_wait(barrier, len(peers))

    def send(src, dst, sent, arrived, peer):
        pltpu.make_async_remote_copy(
            src_ref=src, dst_ref=dst, send_sem=sent, recv_sem=arrived, device_id=peer, device_id_type=MESH
        ).start()

    def take(rows, columns, sem):
        ref = part.at[pl.ds(0, rows * columns // (2 * H))]
        pltpu.make_async_copy(ref, ref, sem).wait()

    def rows_of(start, size):
        return pl.ds(pl.multiple_of(start, 8), size)

    def mine(i):
        return i * chunk + core * half

    def tm_sums(summed, from_core, from_y, from_x, from_x2, from_y2, sent, got):
        columns = summed.shape[1]

        def first(i):
            src = rows_of(i * chunk + (1 - core) * half, half)
            send(summed.at[src], from_core.at[i], sent.at[0], got.at[0, i], other_core)

        def over_1(i):
            take(half, columns, got.at[0, i])
            a, b = mine(i), mine(i) + sub
            own = rows_of(a, half)
            summed[own, :] += from_core[i]
            for d in y_order:
                src = rows_of(a + y_at[d] * (sub // 4), sub // 4)
                send(summed.at[src], from_y.at[i, d - 1], sent.at[1], got.at[1, i], peer_y[d])
            src = rows_of(b + (1 - xl) * (sub // 2), sub // 2)
            send(summed.at[src], from_x.at[i], sent.at[1], got.at[1, i], other_x)

        def over_2(i):
            take(3 * (sub // 4) + sub // 2, columns, got.at[1, i])
            a, b = mine(i) + y * (sub // 4), mine(i) + sub + xl * (sub // 2)
            own = rows_of(a, sub // 4)
            summed[own, :] += from_y[i, 0] + from_y[i, 1] + from_y[i, 2]
            own = rows_of(b, sub // 2)
            summed[own, :] += from_x[i]
            for d in y_order:
                src = rows_of(b + y_at[d] * (sub // 8), sub // 8)
                send(summed.at[src], from_y2.at[i, d - 1], sent.at[2], got.at[2, i], peer_y[d])
            src = rows_of(a + (1 - xl) * (sub // 8), sub // 8)
            send(summed.at[src], from_x2.at[i], sent.at[2], got.at[2, i], other_x)

        def total(i):
            take(4 * (sub // 8), columns, got.at[2, i])
            a, b = owned(i)
            return (
                summed[a, :] + from_x2[i],
                summed[b, :] + (from_y2[i, 0] + from_y2[i, 1] + from_y2[i, 2]),
            )

        return first, over_1, over_2, total

    def owned(i):
        a = rows_of(mine(i) + y * (sub // 4) + xl * (sub // 8), sub // 8)
        b = rows_of(mine(i) + sub + xl * (sub // 2) + y * (sub // 8), sub // 8)
        return a, b

    def tm_gather(gathered, sent, got):
        columns = gathered.shape[1]

        def move(rows, stage, i, peer):
            send(gathered.at[rows], gathered.at[rows], sent.at[stage], got.at[stage, i], peer)

        def start(i):
            a, b = owned(i)
            for d in y_order:
                move(b, 0, i, peer_y[d])
            move(a, 0, i, other_x)

        def spread(i):
            take(4 * (sub // 8), columns, got.at[0, i])
            a = rows_of(mine(i) + y * (sub // 4), sub // 4)
            b = rows_of(mine(i) + sub + xl * (sub // 2), sub // 2)
            for d in y_order:
                move(a, 1, i, peer_y[d])
            move(b, 1, i, other_x)

        def to_core(i):
            take(3 * (sub // 4) + sub // 2, columns, got.at[1, i])
            move(rows_of(mine(i), half), 2, i, other_core)

        def arrive(i):
            take(half, columns, got.at[2, i])

        return start, spread, to_core, arrive

    def multiply_1(i):
        load(i).wait()

        def step(q, _):
            rows = pl.ds(pl.multiple_of(i * chunk + q * 256, 256), 256)
            high, low = split(wide[rows, :])
            s_hi[rows, :] = high
            s_lo[rows, :] = low
            part[rows, :] = dot(high, b_hi[...]) + (dot(high, b_lo[...]) + dot(low, b_hi[...]))
            return 0

        lax.fori_loop(0, chunk // 256, step, 0)

    def place(i, j):
        rows = pl.ds(pl.multiple_of(i * chunk, chunk), chunk)
        columns = pl.ds(pl.multiple_of(j * width, width), width)
        return rows, columns

    def add_back(i, j, h):
        rows, columns = place(i, j)
        terms = p_terms[h]
        value = dot_t(s_hi[rows, columns], terms) + dot_t(s_lo[rows, columns], terms)
        back[h, columns, :] += value[:, :H] + value[:, H:]

    def add_last(i, j, h):
        rows, columns = place(i, j)
        terms = c_terms[h]
        value = dot(s_hi[rows, columns], terms) + dot(s_lo[rows, columns], terms)
        last[h, rows, :] += value[:, :H] + value[:, H:]

    first_1, over_11, over_12, total_1 = tm_sums(part, core_1, y_1, x_1, x2_1, y2_1, sent.at[0], sum_1)
    gathers_1 = [tm_gather(sample.at[h], sent.at[1], gather_1.at[h]) for h in range(2)]

    def begin_1(i, h):
        multiply_1(i)
        first_1(i)

    def finish_1(i, h):
        if h == 0:
            for rows, value in zip(owned(i), total_1(i)):
                sample[0, rows, :], sample[1, rows, :] = scale_halves(value[:, :H], value[:, H:])
        gathers_1[h][0](i)

    def use_1(i, h):
        gathers_1[h][3](i)
        rows = pl.ds(i * chunk, chunk)
        p_terms[h, :, :H], p_terms[h, :, H:] = split(sample[h, rows, :])
        if i < N - 1:
            lax.fori_loop(0, NB, lambda j, _: (add_back(i, j, h), 0)[1], 0)

    def move_b(rows, stage, j, h, peer):
        send(cosample.at[h, rows], cosample.at[h, rows], sent.at[4, stage], got_b.at[h, stage, j], peer)

    def begin_b(j, h):
        add_back(N - 1, j, h)
        src = rows_of(j * width + (1 - xh) * half_b, half_b)
        send(back.at[h, src], from_xh.at[h, j], sent.at[4, 0], got_b.at[h, 0, j], other_xh)

    def over_b(j, h):
        take(half_b, H, got_b.at[h, 0, j])
        a = j * width + xh * half_b
        own = rows_of(a, half_b)
        back[h, own, :] += from_xh[h, j]
        for d in z_order:
            src = rows_of(a + z_at[d] * piece, piece)
            send(back.at[h, src], from_z.at[h, j, d - 1], sent.at[4, 1], got_b.at[h, 1, j], peer_z[d])

    def finish_b(j, h):
        own = rows_of(j * width + xh * half_b + z * piece, piece)
        if h == 0:
            totals = []
            for g in range(2):
                take(7 * piece, H, got_b.at[g, 1, j])
                total = back[g, own, :]
                for d in range(1, NZ):
                    total += from_z[g, j, d - 1]
                totals.append(total)
            cosample[0, own, :], cosample[1, own, :] = scale_halves(*totals)
        for d in z_order:
            move_b(own, 2, j, h, peer_z[d])

    def spread_b(j, h):
        take(7 * piece, H, got_b.at[h, 2, j])
        move_b(rows_of(j * width + xh * half_b, half_b), 3, j, h, other_xh)

    def use_b(j, h):
        take(half_b, H, got_b.at[h, 3, j])
        rows = pl.ds(j * width, width)
        value = cosample[h, rows, :]
        cosample_ref[rows, h * H : (h + 1) * H] = value
        c_terms[h, :, :H], c_terms[h, :, H:] = split(value)
        if j < NB - 1:
            lax.fori_loop(0, N, lambda i, _: (add_last(i, j, h), 0)[1], 0)

    sums_2 = [
        tm_sums(
            last.at[h], core_2.at[h], y_2.at[h], x_2.at[h], x2_2.at[h], y2_2.at[h], sent.at[2], sum_2.at[h]
        )
        for h in range(2)
    ]
    gather_ends = tm_gather(refined_ref, sent.at[3], gather_2)

    def begin_2(i, h):
        add_last(i, NB - 1, h)
        sums_2[h][0](i)

    def finish_2(i, h):
        left, right = sums_2[0][3](i), sums_2[1][3](i)
        for rows, one, two in zip(owned(i), left, right):
            refined_ref[rows, :H], refined_ref[rows, H:] = scale_halves(one, two)
        gather_ends[0](i)

    stages = [
        [begin_1, lambda i, h: over_11(i), lambda i, h: over_12(i), finish_1]
        + [lambda i, h: gathers_1[h][1](i), lambda i, h: gathers_1[h][2](i), use_1],
        [begin_b, over_b, finish_b, spread_b, use_b],
        [begin_2, lambda i, h: sums_2[h][1](i), lambda i, h: sums_2[h][2](i), finish_2]
        + [lambda i, h: gather_ends[1](i), lambda i, h: gather_ends[2](i), lambda i, h: gather_ends[3](i)],
    ]
    for product, stage, at, h in ORDER:
        stages[product][stage](at, h)

    quarter = 5 * (sub // 4)
    for group, counts in enumerate(
        ([half, quarter, sub // 2], [sub // 2, quarter, half], [half, quarter, sub // 2], [sub // 2, quarter, half])
    ):
        for stage, rows in enumerate(counts):
            take(N * rows, 2 * H, sent.at[group, stage])
    for stage, rows in enumerate((half_b, 7 * piece, 7 * piece, half_b)):
        take(NB * rows, 2 * H, sent.at[4, stage])


def local(snapshots, sketch):
    (points, times), k = snapshots.shape, sketch.shape[1]
    chunk, width = points // N, times // NB
    half, sub, half_b = chunk // 2, chunk // 4, width // 2
    vmem = pl.BlockSpec(memory_space=pltpu.VMEM)
    sums = ((N, half), (N, 3, sub // 4), (N, sub // 2), (N, sub // 8), (N, 3, sub // 8))
    return pl.pallas_call(
        kernel,
        name="window",
        out_shape=[jax.ShapeDtypeStruct((points, k), F32), jax.ShapeDtypeStruct((times, k), F32)],
        in_specs=[pl.BlockSpec(memory_space=pl.ANY), vmem],
        out_specs=[vmem, vmem],
        scratch_shapes=[
            pltpu.VMEM((points, times), F32),
            pltpu.VMEM((points, times), BF16),
            pltpu.VMEM((points, times), BF16),
            pltpu.VMEM((times, k), BF16),
            pltpu.VMEM((times, k), BF16),
            pltpu.VMEM((points, k), F32),
            pltpu.VMEM((2, points, H), F32),
            pltpu.VMEM((2, chunk, 2 * H), BF16),
            pltpu.VMEM((2, times, H), F32),
            pltpu.VMEM((2, times, H), F32),
            pltpu.VMEM((2, width, 2 * H), BF16),
            pltpu.VMEM((2, points, H), F32),
            *[pltpu.VMEM((*shape, k), F32) for shape in sums],
            *[pltpu.VMEM((2, *shape, H), F32) for shape in sums],
            pltpu.VMEM((2, NB, half_b, H), F32),
            pltpu.VMEM((2, NB, NZ - 1, half_b // NZ, H), F32),
            pltpu.SemaphoreType.DMA((N,)),
            pltpu.SemaphoreType.DMA((5, 4)),
            pltpu.SemaphoreType.DMA((3, N)),
            pltpu.SemaphoreType.DMA((2, 3, N)),
            pltpu.SemaphoreType.DMA((2, 4, NB)),
            pltpu.SemaphoreType.DMA((2, 3, N)),
            pltpu.SemaphoreType.DMA((3, N)),
        ],
        compiler_params=pltpu.CompilerParams(
            collective_id=0, has_side_effects=True, vmem_limit_bytes=46 << 20
        ),
        cost_estimate=pl.CostEstimate(
            flops=18 * points * times * k, bytes_accessed=4 * points * times, transcendentals=0
        ),
    )(snapshots, sketch)


def solution(mesh):
    return jax.shard_map(
        local,
        mesh=mesh,
        in_specs=(P("space", "tm"), P("tm", None)),
        out_specs=(P("space", None), P("tm", None)),
        check_vma=False,
    )
```

```python
import jax
import jax.numpy as jnp
from jax import lax
from jax.experimental import pallas as pl
from jax.experimental.pallas import tpu as pltpu
from jax.sharding import PartitionSpec as P

EPS = 1e-06
MESH = pl.DeviceIdType.MESH
F32, BF16 = jnp.float32, jnp.bfloat16
NZ, NY = 8, 4
H = 128
N = 4
NB = 4
STEP = 256
ORDER = [
    (0, 0, 0, 0), (0, 0, 1, 0), (0, 1, 0, 0), (0, 0, 2, 0), (0, 1, 1, 0), (0, 0, 3, 0), (0, 1, 2, 0), (0, 2, 0, 0),
    (0, 1, 3, 0), (0, 2, 1, 0), (0, 2, 2, 0), (0, 3, 0, 0), (0, 3, 0, 1), (0, 2, 3, 0), (0, 3, 1, 0), (0, 3, 1, 1),
    (0, 3, 2, 0), (0, 4, 0, 0), (0, 4, 0, 1), (0, 3, 2, 1), (0, 3, 3, 0), (0, 4, 1, 0), (0, 4, 2, 0), (0, 5, 0, 0),
    (0, 4, 1, 1), (0, 5, 0, 1), (0, 3, 3, 1), (0, 4, 3, 0), (0, 6, 0, 0), (0, 5, 1, 0), (0, 6, 0, 1), (0, 5, 2, 0),
    (0, 4, 3, 1), (0, 4, 2, 1), (0, 5, 1, 1), (0, 5, 3, 0), (0, 6, 1, 0), (0, 6, 2, 0), (0, 6, 3, 0), (1, 0, 0, 0),
    (0, 5, 2, 1), (0, 5, 3, 1), (1, 0, 1, 0), (1, 0, 2, 0), (0, 6, 1, 1), (0, 6, 2, 1), (0, 6, 3, 1), (1, 0, 0, 1),
    (1, 1, 0, 0), (1, 0, 1, 1), (1, 1, 1, 0), (1, 0, 2, 1), (1, 1, 2, 0), (1, 0, 3, 1), (1, 1, 0, 1), (1, 0, 3, 0),
    (1, 1, 1, 1), (1, 1, 2, 1), (1, 1, 3, 1), (1, 2, 0, 0), (1, 1, 3, 0), (1, 2, 0, 1), (1, 2, 1, 0), (1, 2, 1, 1),
    (1, 3, 0, 0), (1, 2, 2, 0), (1, 3, 0, 1), (1, 2, 3, 0), (1, 2, 2, 1), (1, 2, 3, 1), (1, 3, 1, 0), (1, 3, 1, 1),
    (1, 4, 0, 0), (1, 3, 2, 0), (1, 4, 0, 1), (1, 3, 3, 0), (1, 4, 1, 0), (1, 3, 2, 1), (1, 4, 1, 1), (1, 3, 3, 1),
    (1, 4, 2, 0), (1, 4, 3, 0), (2, 0, 0, 0), (2, 0, 1, 0), (2, 0, 2, 0), (1, 4, 2, 1), (2, 1, 0, 0), (2, 1, 1, 0),
    (1, 4, 3, 1), (2, 0, 0, 1), (2, 0, 1, 1), (2, 0, 2, 1), (2, 1, 2, 0), (2, 0, 3, 0), (2, 1, 0, 1), (2, 1, 2, 1),
    (2, 0, 3, 1), (2, 1, 1, 1), (2, 1, 3, 0), (2, 1, 3, 1), (2, 2, 0, 1), (2, 2, 0, 0), (2, 2, 2, 0), (2, 2, 2, 1),
    (2, 2, 1, 1), (2, 2, 1, 0), (2, 2, 3, 1), (2, 2, 3, 0), (2, 3, 0, 0), (2, 3, 2, 0), (2, 3, 1, 0), (2, 3, 3, 0),
    (2, 4, 0, 0), (2, 4, 2, 0), (2, 4, 1, 0), (2, 4, 3, 0), (2, 5, 0, 0), (2, 5, 2, 0), (2, 5, 1, 0), (2, 5, 3, 0),
    (2, 6, 0, 0), (2, 6, 1, 0), (2, 6, 2, 0), (2, 6, 3, 0),
]


def split(value):
    high = value.astype(BF16)
    return high, (value - high.astype(F32)).astype(BF16)


def scale_halves(left, right):
    squares = jnp.sum(left * left + right * right, axis=1, keepdims=True)
    factor = lax.rsqrt(squares * (1.0 / (2 * H)) + EPS)
    return left * factor, right * factor


def dot(a, b):
    return jnp.dot(a, b, preferred_element_type=F32)


def dot_t(a, b):
    return lax.dot_general(a, b, (((0,), (0,)), ((), ())), preferred_element_type=F32)


def kernel(
    snap_ref, sketch_ref, refined_ref, cosample_ref,
    wide, sketch, s_hi, s_lo, b_hi, b_lo, part, sample, p_terms, back, cosample, c_terms, last,
    core_1, y_1, x_1, x2_1, y2_1, core_2, y_2, x_2, x2_2, y2_2, from_xh, from_z,
    load_sem, sketch_sem, sent, sum_1, gather_1, got_b, sum_2, gather_2,
):
    points, times = wide.shape
    space, tm = lax.axis_index("space"), lax.axis_index("tm")
    z, xh = space // 2, lax.rem(space, 2)
    xl, y, core = tm // 8, lax.rem(tm // 2, 4), lax.rem(tm, 2)

    def at_tm(xl, y, core):
        return {"space": space, "tm": xl * 8 + y * 2 + core}

    def at_space(z, xh):
        return {"space": z * 2 + xh, "tm": tm}

    other_core, other_x = at_tm(xl, y, 1 - core), at_tm(1 - xl, y, core)
    other_xh = at_space(z, 1 - xh)
    y_at = [lax.rem(y + d, NY) for d in range(NY)]
    z_at = [lax.rem(z + d, NZ) for d in range(NZ)]
    peer_y = [at_tm(xl, y_at[d], core) for d in range(NY)]
    peer_z = [at_space(z_at[d], xh) for d in range(NZ)]
    y_order, z_order = (2, 1, 3), (4, 3, 5, 2, 6, 1, 7)

    chunk, width = points // N, times // NB
    half, sub = chunk // 2, chunk // 4
    half_b = width // 2
    piece = half_b // NZ

    def load(q):
        rows = pl.ds(q * STEP, STEP)
        return pltpu.make_async_copy(snap_ref.at[rows], wide.at[rows], load_sem.at[q])

    load_sketch = pltpu.make_async_copy(sketch_ref, sketch, sketch_sem)
    load_sketch.start()
    for q in range(points // STEP):
        load(q).start()

    barrier = pltpu.get_barrier_semaphore()
    peers = [other_core, other_x, other_xh, *peer_y[1:], *peer_z[1:]]
    for peer in peers:
        pl.semaphore_signal(barrier, inc=1, device_id=peer, device_id_type=MESH)


    def send(src, dst, sent, arrived, peer):
        pltpu.make_async_remote_copy(
            src_ref=src, dst_ref=dst, send_sem=sent, recv_sem=arrived, device_id=peer, device_id_type=MESH
        ).start()

    def take(rows, columns, sem):
        ref = part.at[pl.ds(0, rows * columns // (2 * H))]
        pltpu.make_async_copy(ref, ref, sem).wait()

    def rows_of(start, size):
        return pl.ds(pl.multiple_of(start, 8), size)

    def mine(i):
        return i * chunk + core * half

    def tm_sums(summed, from_core, from_y, from_x, from_x2, from_y2, sent, got):
        columns = summed.shape[1]

        def first(i):
            src = rows_of(i * chunk + (1 - core) * half, half)
            send(summed.at[src], from_core.at[i], sent.at[0], got.at[0, i], other_core)

        def over_1(i):
            take(half, columns, got.at[0, i])
            a, b = mine(i), mine(i) + sub
            own = rows_of(a, half)
            summed[own, :] += from_core[i]
            for d in y_order:
                src = rows_of(a + y_at[d] * (sub // 4), sub // 4)
                send(summed.at[src], from_y.at[i, d - 1], sent.at[1], got.at[1, i], peer_y[d])
            src = rows_of(b + (1 - xl) * (sub // 2), sub // 2)
            send(summed.at[src], from_x.at[i], sent.at[1], got.at[1, i], other_x)

        def over_2(i):
            take(3 * (sub // 4) + sub // 2, columns, got.at[1, i])
            a, b = mine(i) + y * (sub // 4), mine(i) + sub + xl * (sub // 2)
            own = rows_of(a, sub // 4)
            summed[own, :] += from_y[i, 0] + from_y[i, 1] + from_y[i, 2]
            own = rows_of(b, sub // 2)
            summed[own, :] += from_x[i]
            for d in y_order:
                src = rows_of(b + y_at[d] * (sub // 8), sub // 8)
                send(summed.at[src], from_y2.at[i, d - 1], sent.at[2], got.at[2, i], peer_y[d])
            src = rows_of(a + (1 - xl) * (sub // 8), sub // 8)
            send(summed.at[src], from_x2.at[i], sent.at[2], got.at[2, i], other_x)

        def total(i):
            take(4 * (sub // 8), columns, got.at[2, i])
            a, b = owned(i)
            return (
                summed[a, :] + from_x2[i],
                summed[b, :] + (from_y2[i, 0] + from_y2[i, 1] + from_y2[i, 2]),
            )

        return first, over_1, over_2, total

    def owned(i):
        a = rows_of(mine(i) + y * (sub // 4) + xl * (sub // 8), sub // 8)
        b = rows_of(mine(i) + sub + xl * (sub // 2) + y * (sub // 8), sub // 8)
        return a, b

    def tm_gather(gathered, sent, got):
        columns = gathered.shape[1]

        def move(rows, stage, i, peer):
            send(gathered.at[rows], gathered.at[rows], sent.at[stage], got.at[stage, i], peer)

        def start(i):
            a, b = owned(i)
            for d in y_order:
                move(b, 0, i, peer_y[d])
            move(a, 0, i, other_x)

        def spread(i):
            take(4 * (sub // 8), columns, got.at[0, i])
            a = rows_of(mine(i) + y * (sub // 4), sub // 4)
            b = rows_of(mine(i) + sub + xl * (sub // 2), sub // 2)
            for d in y_order:
                move(a, 1, i, peer_y[d])
            move(b, 1, i, other_x)

        def to_core(i):
            take(3 * (sub // 4) + sub // 2, columns, got.at[1, i])
            move(rows_of(mine(i), half), 2, i, other_core)

        def arrive(i):
            take(half, columns, got.at[2, i])

        return start, spread, to_core, arrive

    def multiply_1(i):
        size = STEP if i == 0 else chunk
        for start in range(i * chunk, (i + 1) * chunk, size):
            for q in range(start // STEP, (start + size) // STEP):
                load(q).wait()
            rows = pl.ds(start, size)
            high, low = split(wide[rows, :])
            s_hi[rows, :] = high
            s_lo[rows, :] = low
            part[rows, :] = dot(high, b_hi[...]) + (dot(high, b_lo[...]) + dot(low, b_hi[...]))

    def add_back(i, h):
        rows = pl.ds(i * chunk, chunk)
        terms = p_terms[h]
        value = dot_t(s_hi[rows, :], terms) + dot_t(s_lo[rows, :], terms)
        value = value[:, :H] + value[:, H:]
        back[h] = value if i == 0 else back[h] + value

    def add_last(rows, j, h):
        columns = pl.ds(j * width, width)
        terms = c_terms[h]
        value = dot(s_hi[rows, columns], terms) + dot(s_lo[rows, columns], terms)
        value = value[:, :H] + value[:, H:]
        last[h, rows, :] = value if j == 0 else last[h, rows, :] + value

    first_1, over_11, over_12, total_1 = tm_sums(part, core_1, y_1, x_1, x2_1, y2_1, sent.at[0], sum_1)
    gathers_1 = [tm_gather(sample.at[h], sent.at[1], gather_1.at[h]) for h in range(2)]

    def begin_1(i, h):
        if i == 0:
            load_sketch.wait()
            b_hi[...], b_lo[...] = split(sketch[...])
        multiply_1(i)
        if i == 0:
            pl.semaphore_wait(barrier, len(peers))
        first_1(i)

    def finish_1(i, h):
        if h == 0:
            for rows, value in zip(owned(i), total_1(i)):
                sample[0, rows, :], sample[1, rows, :] = scale_halves(value[:, :H], value[:, H:])
        gathers_1[h][0](i)

    def use_1(i, h):
        gathers_1[h][3](i)
        rows = pl.ds(i * chunk, chunk)
        p_terms[h, :, :H], p_terms[h, :, H:] = split(sample[h, rows, :])
        if i < N - 1:
            add_back(i, h)

    def move_b(rows, stage, j, h, peer):
        send(cosample.at[h, rows], cosample.at[h, rows], sent.at[4, stage], got_b.at[h, stage, j], peer)

    def begin_b(j, h):
        if j == 0:
            add_back(N - 1, h)
        src = rows_of(j * width + (1 - xh) * half_b, half_b)
        send(back.at[h, src], from_xh.at[h, j], sent.at[4, 0], got_b.at[h, 0, j], other_xh)

    def over_b(j, h):
        take(half_b, H, got_b.at[h, 0, j])
        a = j * width + xh * half_b
        own = rows_of(a, half_b)
        back[h, own, :] += from_xh[h, j]
        for d in z_order:
            src = rows_of(a + z_at[d] * piece, piece)
            send(back.at[h, src], from_z.at[h, j, d - 1], sent.at[4, 1], got_b.at[h, 1, j], peer_z[d])

    def finish_b(j, h):
        own = rows_of(j * width + xh * half_b + z * piece, piece)
        if h == 0:
            totals = []
            for g in range(2):
                take(7 * piece, H, got_b.at[g, 1, j])
                total = back[g, own, :]
                for d in range(1, NZ):
                    total += from_z[g, j, d - 1]
                totals.append(total)
            cosample[0, own, :], cosample[1, own, :] = scale_halves(*totals)
        for d in z_order:
            move_b(own, 2, j, h, peer_z[d])

    def spread_b(j, h):
        take(7 * piece, H, got_b.at[h, 2, j])
        move_b(rows_of(j * width + xh * half_b, half_b), 3, j, h, other_xh)

    def use_b(j, h):
        take(half_b, H, got_b.at[h, 3, j])
        rows = pl.ds(j * width, width)
        value = cosample[h, rows, :]
        cosample_ref[rows, h * H : (h + 1) * H] = value
        c_terms[h, :, :H], c_terms[h, :, H:] = split(value)
        if j < NB - 1:
            add_last(pl.ds(0, points), j, h)

    sums_2 = [
        tm_sums(
            last.at[h], core_2.at[h], y_2.at[h], x_2.at[h], x2_2.at[h], y2_2.at[h], sent.at[2], sum_2.at[h]
        )
        for h in range(2)
    ]
    gather_ends = tm_gather(refined_ref, sent.at[3], gather_2)

    def begin_2(i, h):
        if i % (N // 2) == 0:
            add_last(pl.ds(i * chunk, points // 2), NB - 1, h)
        sums_2[h][0](i)

    def finish_2(i, h):
        left, right = sums_2[0][3](i), sums_2[1][3](i)
        for rows, one, two in zip(owned(i), left, right):
            refined_ref[rows, :H], refined_ref[rows, H:] = scale_halves(one, two)
        gather_ends[0](i)

    stages = [
        [begin_1, lambda i, h: over_11(i), lambda i, h: over_12(i), finish_1]
        + [lambda i, h: gathers_1[h][1](i), lambda i, h: gathers_1[h][2](i), use_1],
        [begin_b, over_b, finish_b, spread_b, use_b],
        [begin_2, lambda i, h: sums_2[h][1](i), lambda i, h: sums_2[h][2](i), finish_2]
        + [lambda i, h: gather_ends[1](i), lambda i, h: gather_ends[2](i), lambda i, h: gather_ends[3](i)],
    ]
    for product, stage, at, h in ORDER:
        stages[product][stage](at, h)

    quarter = 5 * (sub // 4)
    for group, counts in enumerate(
        ([half, quarter, sub // 2], [sub // 2, quarter, half], [half, quarter, sub // 2], [sub // 2, quarter, half])
    ):
        for stage, rows in enumerate(counts):
            take(N * rows, 2 * H, sent.at[group, stage])
    for stage, rows in enumerate((half_b, 7 * piece, 7 * piece, half_b)):
        take(NB * rows, 2 * H, sent.at[4, stage])


def local(snapshots, sketch):
    (points, times), k = snapshots.shape, sketch.shape[1]
    chunk, width = points // N, times // NB
    half, sub, half_b = chunk // 2, chunk // 4, width // 2
    vmem = pl.BlockSpec(memory_space=pltpu.VMEM)
    sums = ((N, half), (N, 3, sub // 4), (N, sub // 2), (N, sub // 8), (N, 3, sub // 8))
    return pl.pallas_call(
        kernel,
        name="window",
        out_shape=[jax.ShapeDtypeStruct((points, k), F32), jax.ShapeDtypeStruct((times, k), F32)],
        in_specs=[pl.BlockSpec(memory_space=pl.ANY)] * 2,
        out_specs=[vmem, vmem],
        scratch_shapes=[
            pltpu.VMEM((points, times), F32),
            pltpu.VMEM((times, k), F32),
            pltpu.VMEM((points, times), BF16),
            pltpu.VMEM((points, times), BF16),
            pltpu.VMEM((times, k), BF16),
            pltpu.VMEM((times, k), BF16),
            pltpu.VMEM((points, k), F32),
            pltpu.VMEM((2, points, H), F32),
            pltpu.VMEM((2, chunk, 2 * H), BF16),
            pltpu.VMEM((2, times, H), F32),
            pltpu.VMEM((2, times, H), F32),
            pltpu.VMEM((2, width, 2 * H), BF16),
            pltpu.VMEM((2, points, H), F32),
            *[pltpu.VMEM((*shape, k), F32) for shape in sums],
            *[pltpu.VMEM((2, *shape, H), F32) for shape in sums],
            pltpu.VMEM((2, NB, half_b, H), F32),
            pltpu.VMEM((2, NB, NZ - 1, half_b // NZ, H), F32),
            pltpu.SemaphoreType.DMA((points // STEP,)),
            pltpu.SemaphoreType.DMA,
            pltpu.SemaphoreType.DMA((5, 4)),
            pltpu.SemaphoreType.DMA((3, N)),
            pltpu.SemaphoreType.DMA((2, 3, N)),
            pltpu.SemaphoreType.DMA((2, 4, NB)),
            pltpu.SemaphoreType.DMA((2, 3, N)),
            pltpu.SemaphoreType.DMA((3, N)),
        ],
        compiler_params=pltpu.CompilerParams(
            collective_id=0, has_side_effects=True, vmem_limit_bytes=46 << 20
        ),
        cost_estimate=pl.CostEstimate(
            flops=18 * points * times * k, bytes_accessed=4 * points * times, transcendentals=0
        ),
    )(snapshots, sketch)


def solution(mesh):
    return jax.shard_map(
        local,
        mesh=mesh,
        in_specs=(P("space", "tm"), P("tm", None)),
        out_specs=(P("space", None), P("tm", None)),
        check_vma=False,
    )
```

```python
import jax
import jax.numpy as jnp
from jax import lax
from jax.experimental import pallas as pl
from jax.experimental.pallas import tpu as pltpu
from jax.sharding import PartitionSpec as P

EPS = 1e-06
MESH = pl.DeviceIdType.MESH
F32, BF16 = jnp.float32, jnp.bfloat16
NZ, NY = 8, 4
H = 128
N = 4
NB = 4
STEP = 256
ORDER = [
    (0, 0, 0, 0, 0), (0, 0, 1, 0, 0), (0, 1, 0, 0, 0), (0, 0, 2, 0, 0), (0, 1, 1, 0, 0), (0, 0, 3, 0, 0),
    (0, 1, 2, 0, 0), (0, 2, 0, 0, 1), (0, 2, 0, 0, 0), (0, 1, 3, 0, 0), (0, 2, 1, 0, 0), (0, 2, 1, 0, 1),
    (0, 3, 0, 0, 0), (0, 2, 2, 0, 1), (0, 3, 0, 1, 0), (0, 2, 2, 0, 0), (0, 3, 0, 0, 1), (0, 3, 0, 1, 1),
    (0, 2, 3, 0, 1), (0, 2, 3, 0, 0), (0, 4, 0, 0, 0), (0, 3, 1, 0, 0), (0, 3, 1, 0, 1), (0, 4, 0, 1, 0),
    (0, 3, 2, 0, 0), (0, 3, 2, 1, 0), (0, 3, 1, 1, 0), (0, 3, 2, 0, 1), (0, 4, 0, 0, 1), (0, 3, 1, 1, 1),
    (0, 3, 3, 0, 0), (0, 3, 2, 1, 1), (0, 4, 0, 1, 1), (0, 3, 3, 0, 1), (0, 4, 1, 0, 0), (0, 4, 2, 0, 0),
    (0, 3, 3, 1, 1), (0, 5, 0, 0, 0), (0, 4, 1, 1, 0), (0, 4, 1, 0, 1), (0, 5, 0, 0, 1), (0, 4, 3, 0, 0),
    (0, 4, 2, 1, 0), (0, 5, 0, 1, 0), (0, 4, 2, 0, 1), (0, 3, 3, 1, 0), (0, 5, 0, 1, 1), (0, 4, 2, 1, 1),
    (0, 6, 0, 0, 0), (0, 4, 3, 0, 1), (0, 5, 1, 0, 0), (0, 4, 1, 1, 1), (0, 5, 1, 0, 1), (0, 6, 0, 1, 0),
    (0, 5, 2, 0, 1), (0, 5, 2, 0, 0), (0, 4, 3, 1, 0), (0, 6, 1, 0, 0), (0, 5, 3, 0, 0), (0, 5, 3, 0, 1),
    (0, 4, 3, 1, 1), (0, 5, 1, 1, 0), (0, 6, 2, 0, 0), (0, 5, 1, 1, 1), (0, 6, 3, 0, 0), (1, 0, 0, 0, 0),
    (0, 5, 2, 1, 1), (0, 5, 2, 1, 0), (1, 0, 1, 0, 0), (0, 5, 3, 1, 1), (0, 6, 1, 1, 0), (0, 5, 3, 1, 0),
    (0, 6, 2, 1, 0), (1, 0, 2, 0, 0), (0, 6, 3, 1, 0), (1, 0, 0, 1, 0), (1, 1, 0, 0, 0), (1, 0, 1, 1, 0),
    (1, 1, 1, 0, 0), (1, 0, 2, 1, 0), (1, 0, 3, 0, 0), (1, 1, 2, 0, 0), (1, 0, 3, 1, 0), (1, 1, 0, 1, 0),
    (1, 1, 1, 1, 0), (1, 1, 2, 1, 0), (1, 1, 3, 0, 0), (1, 2, 0, 0, 0), (1, 1, 3, 1, 0), (1, 2, 1, 0, 0),
    (1, 2, 2, 0, 0), (1, 2, 0, 1, 0), (1, 3, 0, 0, 0), (1, 2, 3, 0, 0), (1, 2, 1, 1, 0), (1, 2, 2, 1, 0),
    (1, 3, 1, 0, 0), (1, 3, 2, 0, 0), (1, 4, 0, 0, 0), (1, 3, 0, 1, 0), (1, 2, 3, 1, 0), (1, 3, 3, 0, 0),
    (1, 4, 1, 0, 0), (1, 3, 1, 1, 0), (1, 4, 2, 0, 0), (1, 3, 2, 1, 0), (1, 4, 0, 1, 0), (1, 4, 3, 0, 0),
    (1, 3, 3, 1, 0), (2, 0, 0, 0, 0), (2, 0, 1, 0, 0), (2, 0, 2, 0, 0), (2, 0, 3, 0, 0), (1, 4, 1, 1, 0),
    (2, 1, 0, 0, 0), (1, 4, 2, 1, 0), (2, 1, 3, 0, 0), (2, 1, 1, 0, 0), (1, 4, 3, 1, 0), (2, 0, 0, 1, 0),
    (2, 1, 2, 0, 0), (2, 0, 1, 1, 0), (2, 0, 2, 1, 0), (2, 2, 0, 0, 1), (2, 0, 3, 1, 0), (2, 1, 0, 1, 0),
    (2, 1, 1, 1, 0), (2, 1, 2, 1, 0), (2, 1, 3, 1, 0), (2, 2, 0, 1, 1), (2, 2, 1, 0, 1), (2, 2, 1, 0, 0),
    (2, 2, 0, 0, 0), (2, 2, 0, 1, 0), (2, 2, 1, 1, 1), (2, 2, 2, 0, 1), (2, 2, 2, 1, 1), (2, 2, 2, 0, 0),
    (2, 2, 3, 0, 1), (2, 2, 1, 1, 0), (2, 2, 2, 1, 0), (2, 2, 3, 1, 1), (2, 2, 3, 0, 0), (2, 2, 3, 1, 0),
    (2, 3, 0, 0, 1), (2, 3, 0, 0, 0), (2, 3, 1, 0, 1), (2, 3, 1, 0, 0), (2, 3, 2, 0, 1), (2, 3, 3, 0, 0),
    (2, 3, 3, 0, 1), (2, 3, 2, 0, 0), (2, 4, 0, 0, 0), (2, 4, 0, 0, 1), (2, 4, 1, 0, 0), (2, 4, 3, 0, 0),
    (2, 4, 2, 0, 1), (2, 4, 2, 0, 0), (2, 4, 3, 0, 1), (2, 4, 1, 0, 1), (2, 5, 0, 0, 0), (2, 5, 3, 0, 1),
    (2, 5, 1, 0, 0), (2, 5, 3, 0, 0), (2, 5, 2, 0, 1), (2, 5, 0, 0, 1), (2, 5, 1, 0, 1), (2, 5, 2, 0, 0),
    (2, 6, 3, 0, 0), (2, 6, 0, 0, 0), (2, 6, 1, 0, 0), (2, 6, 2, 0, 0),
]


def split(value):
    high = value.astype(BF16)
    return high, (value - high.astype(F32)).astype(BF16)


def scale_halves(left, right):
    squares = jnp.sum(left * left + right * right, axis=1, keepdims=True)
    factor = lax.rsqrt(squares * (1.0 / (2 * H)) + EPS)
    return left * factor, right * factor


def dot(a, b):
    return jnp.dot(a, b, preferred_element_type=F32)


def dot_t(a, b):
    return lax.dot_general(a, b, (((0,), (0,)), ((), ())), preferred_element_type=F32)


def kernel(
    snap_ref, sketch_ref, refined_ref, cosample_ref,
    wide, sketch, s_hi, s_lo, b_hi, b_lo, part, sample, p_terms, back, cosample, c_terms, last,
    core_1, y_1, x_1, x2_1, y2_1, core_2, y_2, x_2, x2_2, y2_2, from_xh, from_z,
    load_sem, sketch_sem, sent, sum_1, gather_1, got_b, sum_2, gather_2,
):
    points, times = wide.shape
    space, tm = lax.axis_index("space"), lax.axis_index("tm")
    z, xh = space // 2, lax.rem(space, 2)
    xl, y, core = tm // 8, lax.rem(tm // 2, 4), lax.rem(tm, 2)

    def at_tm(xl, y, core):
        return {"space": space, "tm": xl * 8 + y * 2 + core}

    def at_space(z, xh):
        return {"space": z * 2 + xh, "tm": tm}

    other_core, other_x = at_tm(xl, y, 1 - core), at_tm(1 - xl, y, core)
    other_xh = at_space(z, 1 - xh)
    y_at = [lax.rem(y + d, NY) for d in range(NY)]
    z_at = [lax.rem(z + d, NZ) for d in range(NZ)]
    peer_y = [at_tm(xl, y_at[d], core) for d in range(NY)]
    peer_z = [at_space(z_at[d], xh) for d in range(NZ)]
    y_order, z_order = (2, 1, 3), (4, 3, 5, 2, 6, 1, 7)

    chunk, width = points // N, times // NB
    half, sub = chunk // 2, chunk // 4
    half_b = width // 2
    piece = half_b // NZ

    def load(q):
        rows = pl.ds(q * STEP, STEP)
        return pltpu.make_async_copy(snap_ref.at[rows], wide.at[rows], load_sem.at[q])

    load_sketch = pltpu.make_async_copy(sketch_ref, sketch, sketch_sem)
    load_sketch.start()
    for q in range(points // STEP):
        load(q).start()

    barrier = pltpu.get_barrier_semaphore()
    peers = [other_core, other_x, other_xh, *peer_y[1:], *peer_z[1:]]
    for peer in peers:
        pl.semaphore_signal(barrier, inc=1, device_id=peer, device_id_type=MESH)


    def send(src, dst, sent, arrived, peer):
        pltpu.make_async_remote_copy(
            src_ref=src, dst_ref=dst, send_sem=sent, recv_sem=arrived, device_id=peer, device_id_type=MESH
        ).start()

    def take(rows, columns, sem):
        ref = part.at[pl.ds(0, rows * columns // (2 * H))]
        pltpu.make_async_copy(ref, ref, sem).wait()

    def rows_of(start, size):
        return pl.ds(pl.multiple_of(start, 8), size)

    def mine(i):
        return i * chunk + core * half

    def tm_sums(summed, from_core, from_y, from_x, from_x2, from_y2, sent, got):
        columns = summed.shape[1]

        def first(i):
            src = rows_of(i * chunk + (1 - core) * half, half)
            send(summed.at[src], from_core.at[i], sent.at[0], got.at[0, i], other_core)

        def over_1(i):
            take(half, columns, got.at[0, i])
            a, b = mine(i), mine(i) + sub
            own = rows_of(a, half)
            summed[own, :] += from_core[i]
            for d in y_order:
                src = rows_of(a + y_at[d] * (sub // 4), sub // 4)
                send(summed.at[src], from_y.at[i, d - 1], sent.at[1], got.at[1, i], peer_y[d])
            src = rows_of(b + (1 - xl) * (sub // 2), sub // 2)
            send(summed.at[src], from_x.at[i], sent.at[1], got.at[2, i], other_x)

        def over_2(i, p):
            if p == 0:
                take(3 * (sub // 4), columns, got.at[1, i])
                a = mine(i) + y * (sub // 4)
                own = rows_of(a, sub // 4)
                summed[own, :] += from_y[i, 0] + from_y[i, 1] + from_y[i, 2]
                src = rows_of(a + (1 - xl) * (sub // 8), sub // 8)
                send(summed.at[src], from_x2.at[i], sent.at[2], got.at[3, i], other_x)
            else:
                take(sub // 2, columns, got.at[2, i])
                b = mine(i) + sub + xl * (sub // 2)
                own = rows_of(b, sub // 2)
                summed[own, :] += from_x[i]
                for d in y_order:
                    src = rows_of(b + y_at[d] * (sub // 8), sub // 8)
                    send(summed.at[src], from_y2.at[i, d - 1], sent.at[2], got.at[4, i], peer_y[d])

        def total(i, p):
            own = owned(i, p)
            if p == 0:
                take(sub // 8, columns, got.at[3, i])
                return summed[own, :] + from_x2[i]
            take(3 * (sub // 8), columns, got.at[4, i])
            return summed[own, :] + (from_y2[i, 0] + from_y2[i, 1] + from_y2[i, 2])

        return first, over_1, over_2, total

    def owned(i, p):
        if p == 0:
            return rows_of(mine(i) + y * (sub // 4) + xl * (sub // 8), sub // 8)
        return rows_of(mine(i) + sub + xl * (sub // 2) + y * (sub // 8), sub // 8)

    def tm_gather(gathered, sent, got):
        columns = gathered.shape[1]

        def move(rows, stage, place, i, peer):
            send(gathered.at[rows], gathered.at[rows], sent.at[stage], got.at[place, i], peer)

        def start(i, p):
            own = owned(i, p)
            if p == 0:
                move(own, 0, 0, i, other_x)
            else:
                for d in y_order:
                    move(own, 0, 1, i, peer_y[d])

        def spread(i, p):
            if p == 0:
                take(sub // 8, columns, got.at[0, i])
                rows = rows_of(mine(i) + y * (sub // 4), sub // 4)
                for d in y_order:
                    move(rows, 1, 2, i, peer_y[d])
            else:
                take(3 * (sub // 8), columns, got.at[1, i])
                move(rows_of(mine(i) + sub + xl * (sub // 2), sub // 2), 1, 3, i, other_x)

        def to_core(i, p):
            if p == 0:
                take(3 * (sub // 4), columns, got.at[2, i])
            else:
                take(sub // 2, columns, got.at[3, i])
            move(rows_of(mine(i) + p * sub, sub), 2, 4, i, other_core)

        def arrive(i):
            take(half, columns, got.at[4, i])

        return start, spread, to_core, arrive

    def multiply_1(i):
        size = STEP if i == 0 else chunk
        for start in range(i * chunk, (i + 1) * chunk, size):
            for q in range(start // STEP, (start + size) // STEP):
                load(q).wait()
            rows = pl.ds(start, size)
            high, low = split(wide[rows, :])
            s_hi[rows, :] = high
            s_lo[rows, :] = low
            part[rows, :] = dot(high, b_hi[...]) + (dot(high, b_lo[...]) + dot(low, b_hi[...]))

    def add_back(i, h):
        rows = pl.ds(i * chunk, chunk)
        terms = p_terms[h]
        value = dot_t(s_hi[rows, :], terms) + dot_t(s_lo[rows, :], terms)
        value = value[:, :H] + value[:, H:]
        back[h] = value if i == 0 else back[h] + value

    def add_last(rows, j, h):
        columns = pl.ds(j * width, width)
        terms = c_terms[h]
        value = dot(s_hi[rows, columns], terms) + dot(s_lo[rows, columns], terms)
        value = value[:, :H] + value[:, H:]
        last[h, rows, :] = value if j == 0 else last[h, rows, :] + value

    first_1, over_11, over_12, total_1 = tm_sums(part, core_1, y_1, x_1, x2_1, y2_1, sent.at[0], sum_1)
    gathers_1 = [tm_gather(sample.at[h], sent.at[1], gather_1.at[h]) for h in range(2)]

    def begin_1(i, h, p):
        if i == 0:
            load_sketch.wait()
            b_hi[...], b_lo[...] = split(sketch[...])
        multiply_1(i)
        if i == 0:
            pl.semaphore_wait(barrier, len(peers))
        first_1(i)

    def finish_1(i, h, p):
        if h == 0:
            rows, value = owned(i, p), total_1(i, p)
            sample[0, rows, :], sample[1, rows, :] = scale_halves(value[:, :H], value[:, H:])
        gathers_1[h][0](i, p)

    def use_1(i, h, p):
        gathers_1[h][3](i)
        rows = pl.ds(i * chunk, chunk)
        p_terms[h, :, :H], p_terms[h, :, H:] = split(sample[h, rows, :])
        if i < N - 1:
            add_back(i, h)

    def move_b(rows, stage, j, h, peer):
        send(cosample.at[h, rows], cosample.at[h, rows], sent.at[4, stage], got_b.at[h, stage, j], peer)

    def begin_b(j, h, p):
        if j == 0:
            add_back(N - 1, h)
        src = rows_of(j * width + (1 - xh) * half_b, half_b)
        send(back.at[h, src], from_xh.at[h, j], sent.at[4, 0], got_b.at[h, 0, j], other_xh)

    def over_b(j, h, p):
        take(half_b, H, got_b.at[h, 0, j])
        a = j * width + xh * half_b
        own = rows_of(a, half_b)
        back[h, own, :] += from_xh[h, j]
        for d in z_order:
            src = rows_of(a + z_at[d] * piece, piece)
            send(back.at[h, src], from_z.at[h, j, d - 1], sent.at[4, 1], got_b.at[h, 1, j], peer_z[d])

    def finish_b(j, h, p):
        own = rows_of(j * width + xh * half_b + z * piece, piece)
        if h == 0:
            totals = []
            for g in range(2):
                take(7 * piece, H, got_b.at[g, 1, j])
                total = back[g, own, :]
                for d in range(1, NZ):
                    total += from_z[g, j, d - 1]
                totals.append(total)
            cosample[0, own, :], cosample[1, own, :] = scale_halves(*totals)
        for d in z_order:
            move_b(own, 2, j, h, peer_z[d])

    def spread_b(j, h, p):
        take(7 * piece, H, got_b.at[h, 2, j])
        move_b(rows_of(j * width + xh * half_b, half_b), 3, j, h, other_xh)

    def use_b(j, h, p):
        take(half_b, H, got_b.at[h, 3, j])
        rows = pl.ds(j * width, width)
        value = cosample[h, rows, :]
        cosample_ref[rows, h * H : (h + 1) * H] = value
        c_terms[h, :, :H], c_terms[h, :, H:] = split(value)
        if j < NB - 1:
            add_last(pl.ds(0, points), j, h)

    sums_2 = [
        tm_sums(
            last.at[h], core_2.at[h], y_2.at[h], x_2.at[h], x2_2.at[h], y2_2.at[h], sent.at[2], sum_2.at[h]
        )
        for h in range(2)
    ]
    gather_ends = tm_gather(refined_ref, sent.at[3], gather_2)

    def begin_2(i, h, p):
        if i % (N // 2) == 0:
            add_last(pl.ds(i * chunk, points // 2), NB - 1, h)
        sums_2[h][0](i)

    def finish_2(i, h, p):
        rows = owned(i, p)
        refined_ref[rows, :H], refined_ref[rows, H:] = scale_halves(sums_2[0][3](i, p), sums_2[1][3](i, p))
        gather_ends[0](i, p)

    stages = [
        [begin_1, lambda i, h, p: over_11(i), lambda i, h, p: over_12(i, p), finish_1]
        + [lambda i, h, p: gathers_1[h][1](i, p), lambda i, h, p: gathers_1[h][2](i, p), use_1],
        [begin_b, over_b, finish_b, spread_b, use_b],
        [begin_2, lambda i, h, p: sums_2[h][1](i), lambda i, h, p: sums_2[h][2](i, p), finish_2]
        + [lambda i, h, p: gather_ends[1](i, p), lambda i, h, p: gather_ends[2](i, p)]
        + [lambda i, h, p: gather_ends[3](i)],
    ]
    for product, stage, at, h, p in ORDER:
        stages[product][stage](at, h, p)

    quarter = 5 * (sub // 4)
    for group, counts in enumerate(
        ([half, quarter, sub // 2], [sub // 2, quarter, half], [half, quarter, sub // 2], [sub // 2, quarter, half])
    ):
        for stage, rows in enumerate(counts):
            take(N * rows, 2 * H, sent.at[group, stage])
    for stage, rows in enumerate((half_b, 7 * piece, 7 * piece, half_b)):
        take(NB * rows, 2 * H, sent.at[4, stage])


def local(snapshots, sketch):
    (points, times), k = snapshots.shape, sketch.shape[1]
    chunk, width = points // N, times // NB
    half, sub, half_b = chunk // 2, chunk // 4, width // 2
    vmem = pl.BlockSpec(memory_space=pltpu.VMEM)
    sums = ((N, half), (N, 3, sub // 4), (N, sub // 2), (N, sub // 8), (N, 3, sub // 8))
    return pl.pallas_call(
        kernel,
        name="window",
        out_shape=[jax.ShapeDtypeStruct((points, k), F32), jax.ShapeDtypeStruct((times, k), F32)],
        in_specs=[pl.BlockSpec(memory_space=pl.ANY)] * 2,
        out_specs=[vmem, vmem],
        scratch_shapes=[
            pltpu.VMEM((points, times), F32),
            pltpu.VMEM((times, k), F32),
            pltpu.VMEM((points, times), BF16),
            pltpu.VMEM((points, times), BF16),
            pltpu.VMEM((times, k), BF16),
            pltpu.VMEM((times, k), BF16),
            pltpu.VMEM((points, k), F32),
            pltpu.VMEM((2, points, H), F32),
            pltpu.VMEM((2, chunk, 2 * H), BF16),
            pltpu.VMEM((2, times, H), F32),
            pltpu.VMEM((2, times, H), F32),
            pltpu.VMEM((2, width, 2 * H), BF16),
            pltpu.VMEM((2, points, H), F32),
            *[pltpu.VMEM((*shape, k), F32) for shape in sums],
            *[pltpu.VMEM((2, *shape, H), F32) for shape in sums],
            pltpu.VMEM((2, NB, half_b, H), F32),
            pltpu.VMEM((2, NB, NZ - 1, half_b // NZ, H), F32),
            pltpu.SemaphoreType.DMA((points // STEP,)),
            pltpu.SemaphoreType.DMA,
            pltpu.SemaphoreType.DMA((5, 4)),
            pltpu.SemaphoreType.DMA((5, N)),
            pltpu.SemaphoreType.DMA((2, 5, N)),
            pltpu.SemaphoreType.DMA((2, 4, NB)),
            pltpu.SemaphoreType.DMA((2, 5, N)),
            pltpu.SemaphoreType.DMA((5, N)),
        ],
        compiler_params=pltpu.CompilerParams(
            collective_id=0, has_side_effects=True, vmem_limit_bytes=46 << 20
        ),
        cost_estimate=pl.CostEstimate(
            flops=18 * points * times * k, bytes_accessed=4 * points * times, transcendentals=0
        ),
    )(snapshots, sketch)


def solution(mesh):
    return jax.shard_map(
        local,
        mesh=mesh,
        in_specs=(P("space", "tm"), P("tm", None)),
        out_specs=(P("space", None), P("tm", None)),
        check_vma=False,
    )
```

```python
import jax
import jax.numpy as jnp
from jax import lax
from jax.experimental import pallas as pl
from jax.experimental.pallas import tpu as pltpu
from jax.sharding import PartitionSpec as P

EPS = 1e-06
MESH = pl.DeviceIdType.MESH
F32, BF16 = jnp.float32, jnp.bfloat16
NZ, NY = 8, 4
H = 128
N = 4
NB = 4
STEP = 256
PIECES = 2
ORDER = [
    (0, 0, 0, 0, 0), (0, 0, 1, 0, 0), (0, 1, 0, 0, 0), (0, 0, 2, 0, 0), (0, 1, 1, 0, 0), (0, 0, 3, 0, 0),
    (0, 1, 2, 0, 0), (0, 2, 0, 0, 1), (0, 2, 0, 0, 0), (0, 1, 3, 0, 0), (0, 2, 1, 0, 0), (0, 2, 1, 0, 1),
    (0, 3, 0, 0, 0), (0, 2, 2, 0, 1), (0, 3, 0, 1, 0), (0, 2, 2, 0, 0), (0, 3, 0, 0, 1), (0, 3, 0, 1, 1),
    (0, 2, 3, 0, 1), (0, 2, 3, 0, 0), (0, 4, 0, 0, 0), (0, 3, 1, 0, 0), (0, 3, 1, 0, 1), (0, 4, 0, 1, 0),
    (0, 3, 2, 0, 0), (0, 3, 2, 1, 0), (0, 3, 1, 1, 0), (0, 3, 2, 0, 1), (0, 4, 0, 0, 1), (0, 3, 1, 1, 1),
    (0, 3, 3, 0, 0), (0, 3, 2, 1, 1), (0, 4, 0, 1, 1), (0, 3, 3, 0, 1), (0, 4, 1, 0, 0), (0, 4, 2, 0, 0),
    (0, 3, 3, 1, 1), (0, 5, 0, 0, 0), (0, 4, 1, 1, 0), (0, 4, 1, 0, 1), (0, 5, 0, 0, 1), (0, 4, 3, 0, 0),
    (0, 4, 2, 1, 0), (0, 5, 0, 1, 0), (0, 4, 2, 0, 1), (0, 3, 3, 1, 0), (0, 5, 0, 1, 1), (0, 4, 2, 1, 1),
    (0, 6, 0, 0, 0), (0, 4, 3, 0, 1), (0, 5, 1, 0, 0), (0, 4, 1, 1, 1), (0, 5, 1, 0, 1), (0, 6, 0, 1, 0),
    (0, 5, 2, 0, 1), (0, 5, 2, 0, 0), (0, 4, 3, 1, 0), (0, 6, 1, 0, 0), (0, 5, 3, 0, 0), (0, 5, 3, 0, 1),
    (0, 4, 3, 1, 1), (0, 5, 1, 1, 0), (0, 6, 2, 0, 0), (0, 5, 1, 1, 1), (0, 6, 3, 0, 0), (1, 0, 0, 0, 0),
    (0, 5, 2, 1, 1), (0, 5, 2, 1, 0), (1, 0, 1, 0, 0), (0, 5, 3, 1, 1), (0, 6, 1, 1, 0), (0, 5, 3, 1, 0),
    (0, 6, 2, 1, 0), (1, 0, 2, 0, 0), (0, 6, 3, 1, 0), (1, 0, 0, 1, 0), (1, 1, 0, 0, 0), (1, 0, 1, 1, 0),
    (1, 1, 1, 0, 0), (1, 0, 2, 1, 0), (1, 0, 3, 0, 0), (1, 1, 2, 0, 0), (1, 0, 3, 1, 0), (1, 1, 0, 1, 0),
    (1, 1, 1, 1, 0), (1, 1, 2, 1, 0), (1, 1, 3, 0, 0), (1, 2, 0, 0, 0), (1, 1, 3, 1, 0), (1, 2, 1, 0, 0),
    (1, 2, 2, 0, 0), (1, 2, 0, 1, 0), (1, 3, 0, 0, 0), (1, 2, 3, 0, 0), (1, 2, 1, 1, 0), (1, 2, 2, 1, 0),
    (1, 3, 1, 0, 0), (1, 3, 2, 0, 0), (1, 4, 0, 0, 0), (1, 3, 0, 1, 0), (1, 2, 3, 1, 0), (1, 3, 3, 0, 0),
    (1, 4, 1, 0, 0), (1, 3, 1, 1, 0), (1, 4, 2, 0, 0), (1, 3, 2, 1, 0), (1, 4, 0, 1, 0), (1, 4, 3, 0, 0),
    (1, 3, 3, 1, 0), (2, 0, 0, 0, 0), (2, 0, 1, 0, 0), (2, 0, 2, 0, 0), (2, 0, 3, 0, 0), (1, 4, 1, 1, 0),
    (2, 1, 0, 0, 0), (1, 4, 2, 1, 0), (2, 1, 3, 0, 0), (2, 1, 1, 0, 0), (1, 4, 3, 1, 0), (2, 0, 0, 1, 0),
    (2, 1, 2, 0, 0), (2, 0, 1, 1, 0), (2, 0, 2, 1, 0), (2, 2, 0, 0, 1), (2, 0, 3, 1, 0), (2, 1, 0, 1, 0),
    (2, 1, 1, 1, 0), (2, 1, 2, 1, 0), (2, 1, 3, 1, 0), (2, 2, 0, 1, 1), (2, 2, 1, 0, 1), (2, 2, 1, 0, 0),
    (2, 2, 0, 0, 0), (2, 2, 0, 1, 0), (2, 2, 1, 1, 1), (2, 2, 2, 0, 1), (2, 2, 2, 1, 1), (2, 2, 2, 0, 0),
    (2, 2, 3, 0, 1), (2, 2, 1, 1, 0), (2, 2, 2, 1, 0), (2, 2, 3, 1, 1), (2, 2, 3, 0, 0), (2, 2, 3, 1, 0),
    (2, 3, 0, 0, 1), (2, 3, 0, 0, 0), (2, 3, 1, 0, 1), (2, 3, 1, 0, 0), (2, 3, 2, 0, 1), (2, 3, 3, 0, 0),
    (2, 3, 3, 0, 1), (2, 3, 2, 0, 0), (2, 4, 0, 0, 0), (2, 4, 0, 0, 1), (2, 4, 1, 0, 0), (2, 4, 3, 0, 0),
    (2, 4, 2, 0, 1), (2, 4, 2, 0, 0), (2, 4, 3, 0, 1), (2, 4, 1, 0, 1), (2, 5, 0, 0, 0), (2, 5, 3, 0, 1),
    (2, 5, 1, 0, 0), (2, 5, 3, 0, 0), (2, 5, 2, 0, 1), (2, 5, 0, 0, 1), (2, 5, 1, 0, 1), (2, 5, 2, 0, 0),
    (2, 6, 3, 0, 0), (2, 6, 0, 0, 0), (2, 6, 1, 0, 0), (2, 6, 2, 0, 0),
]


def split(value):
    high = value.astype(BF16)
    return high, (value - high.astype(F32)).astype(BF16)


def scale_halves(left, right):
    squares = jnp.sum(left * left + right * right, axis=1, keepdims=True)
    factor = lax.rsqrt(squares * (1.0 / (2 * H)) + EPS)
    return left * factor, right * factor


def dot(a, b):
    return jnp.dot(a, b, preferred_element_type=F32)


def dot_t(a, b):
    return lax.dot_general(a, b, (((0,), (0,)), ((), ())), preferred_element_type=F32)


def kernel(
    snap_ref, sketch_ref, refined_ref, cosample_ref,
    wide, sketch, s_hi, s_lo, b_hi, b_lo, part, sample, p_terms, back, cosample, c_terms, last,
    core_1, y_1, x_1, x2_1, y2_1, core_2, y_2, x_2, x2_2, y2_2, from_xh, from_z,
    load_sem, sketch_sem, sent, sum_1, gather_1, got_b, sum_2, gather_2,
):
    points, times = wide.shape
    space, tm = lax.axis_index("space"), lax.axis_index("tm")
    z, xh = space // 2, lax.rem(space, 2)
    xl, y, core = tm // 8, lax.rem(tm // 2, 4), lax.rem(tm, 2)

    def at_tm(xl, y, core):
        return {"space": space, "tm": xl * 8 + y * 2 + core}

    def at_space(z, xh):
        return {"space": z * 2 + xh, "tm": tm}

    other_core, other_x = at_tm(xl, y, 1 - core), at_tm(1 - xl, y, core)
    other_xh = at_space(z, 1 - xh)
    y_at = [lax.rem(y + d, NY) for d in range(NY)]
    z_at = [lax.rem(z + d, NZ) for d in range(NZ)]
    peer_y = [at_tm(xl, y_at[d], core) for d in range(NY)]
    peer_z = [at_space(z_at[d], xh) for d in range(NZ)]
    y_order, z_order = (2, 1, 3), (4, 3, 5, 2, 6, 1, 7)

    chunk, width = points // N, times // NB
    half, sub = chunk // 2, chunk // 4
    half_b = width // 2
    piece = half_b // NZ

    def load(q):
        rows = pl.ds(q * STEP, STEP)
        return pltpu.make_async_copy(snap_ref.at[rows], wide.at[rows], load_sem.at[q])

    load_sketch = pltpu.make_async_copy(sketch_ref, sketch, sketch_sem)
    load_sketch.start()
    for q in range(points // STEP):
        load(q).start()

    barrier = pltpu.get_barrier_semaphore()
    peers = [other_core, other_x, other_xh, *peer_y[1:], *peer_z[1:]]
    for peer in peers:
        pl.semaphore_signal(barrier, inc=1, device_id=peer, device_id_type=MESH)


    def send(src, dst, sent, arrived, peer):
        pltpu.make_async_remote_copy(
            src_ref=src, dst_ref=dst, send_sem=sent, recv_sem=arrived, device_id=peer, device_id_type=MESH
        ).start()

    def take(rows, columns, sem):
        ref = part.at[pl.ds(0, rows * columns // (2 * H))]
        pltpu.make_async_copy(ref, ref, sem).wait()

    def rows_of(start, size):
        return pl.ds(pl.multiple_of(start, 8), size)

    def mine(i):
        return i * chunk + core * half

    def tm_sums(summed, from_core, from_y, from_x, from_x2, from_y2, sent, got):
        columns = summed.shape[1]

        def first(i):
            src = rows_of(i * chunk + (1 - core) * half, half)
            send(summed.at[src], from_core.at[i], sent.at[0], got.at[0, i], other_core)

        def over_1(i):
            take(half, columns, got.at[0, i])
            a, b = mine(i), mine(i) + sub
            own = rows_of(a, half)
            summed[own, :] += from_core[i]
            for d in y_order:
                src = rows_of(a + y_at[d] * (sub // 4), sub // 4)
                send(summed.at[src], from_y.at[i, d - 1], sent.at[1], got.at[1, i], peer_y[d])
            src = rows_of(b + (1 - xl) * (sub // 2), sub // 2)
            send(summed.at[src], from_x.at[i], sent.at[1], got.at[2, i], other_x)

        def over_2(i, p):
            if p == 0:
                take(3 * (sub // 4), columns, got.at[1, i])
                a = mine(i) + y * (sub // 4)
                own = rows_of(a, sub // 4)
                summed[own, :] += from_y[i, 0] + from_y[i, 1] + from_y[i, 2]
                src = rows_of(a + (1 - xl) * (sub // 8), sub // 8)
                send(summed.at[src], from_x2.at[i], sent.at[2], got.at[3, i], other_x)
            else:
                take(sub // 2, columns, got.at[2, i])
                b = mine(i) + sub + xl * (sub // 2)
                own = rows_of(b, sub // 2)
                summed[own, :] += from_x[i]
                for d in y_order:
                    src = rows_of(b + y_at[d] * (sub // 8), sub // 8)
                    send(summed.at[src], from_y2.at[i, d - 1], sent.at[2], got.at[4, i], peer_y[d])

        def total(i, p):
            own = owned(i, p)
            if p == 0:
                take(sub // 8, columns, got.at[3, i])
                return summed[own, :] + from_x2[i]
            take(3 * (sub // 8), columns, got.at[4, i])
            return summed[own, :] + (from_y2[i, 0] + from_y2[i, 1] + from_y2[i, 2])

        return first, over_1, over_2, total

    def owned(i, p):
        if p == 0:
            return rows_of(mine(i) + y * (sub // 4) + xl * (sub // 8), sub // 8)
        return rows_of(mine(i) + sub + xl * (sub // 2) + y * (sub // 8), sub // 8)

    def tm_gather(gathered, sent, got):
        columns = gathered.shape[1]

        def move(rows, stage, place, i, peer):
            send(gathered.at[rows], gathered.at[rows], sent.at[stage], got.at[place, i], peer)

        def start(i, p):
            own = owned(i, p)
            if p == 0:
                move(own, 0, 0, i, other_x)
            else:
                for d in y_order:
                    move(own, 0, 1, i, peer_y[d])

        def spread(i, p):
            if p == 0:
                take(sub // 8, columns, got.at[0, i])
                rows = rows_of(mine(i) + y * (sub // 4), sub // 4)
                for d in y_order:
                    move(rows, 1, 2, i, peer_y[d])
            else:
                take(3 * (sub // 8), columns, got.at[1, i])
                move(rows_of(mine(i) + sub + xl * (sub // 2), sub // 2), 1, 3, i, other_x)

        def to_core(i, p):
            if p == 0:
                take(3 * (sub // 4), columns, got.at[2, i])
            else:
                take(sub // 2, columns, got.at[3, i])
            move(rows_of(mine(i) + p * sub, sub), 2, 4, i, other_core)

        def arrive(i):
            take(half, columns, got.at[4, i])

        return start, spread, to_core, arrive

    def multiply_1(i):
        size = STEP if i == 0 else chunk
        for start in range(i * chunk, (i + 1) * chunk, size):
            for q in range(start // STEP, (start + size) // STEP):
                load(q).wait()
            rows = pl.ds(start, size)
            high, low = split(wide[rows, :])
            s_hi[rows, :] = high
            s_lo[rows, :] = low
            part[rows, :] = dot(high, b_hi[...]) + (dot(high, b_lo[...]) + dot(low, b_hi[...]))

    def add_back(i, h):
        rows = pl.ds(i * chunk, chunk)
        terms = p_terms[h]
        value = dot_t(s_hi[rows, :], terms) + dot_t(s_lo[rows, :], terms)
        value = value[:, :H] + value[:, H:]
        back[h] = value if i == 0 else back[h] + value

    def add_last(rows, j, h):
        columns = pl.ds(j * width, width)
        terms = c_terms[h]
        value = dot(s_hi[rows, columns], terms) + dot(s_lo[rows, columns], terms)
        value = value[:, :H] + value[:, H:]
        last[h, rows, :] = value if j == 0 else last[h, rows, :] + value

    first_1, over_11, over_12, total_1 = tm_sums(part, core_1, y_1, x_1, x2_1, y2_1, sent.at[0], sum_1)
    gathers_1 = [tm_gather(sample.at[h], sent.at[1], gather_1.at[h]) for h in range(2)]

    def begin_1(i, h, p):
        if i == 0:
            load_sketch.wait()
            b_hi[...], b_lo[...] = split(sketch[...])
        multiply_1(i)
        if i == 0:
            pl.semaphore_wait(barrier, len(peers))
        first_1(i)

    def finish_1(i, h, p):
        if h == 0:
            rows, value = owned(i, p), total_1(i, p)
            sample[0, rows, :], sample[1, rows, :] = scale_halves(value[:, :H], value[:, H:])
        gathers_1[h][0](i, p)

    def use_1(i, h, p):
        gathers_1[h][3](i)
        rows = pl.ds(i * chunk, chunk)
        p_terms[h, :, :H], p_terms[h, :, H:] = split(sample[h, rows, :])
        if i < N - 1:
            add_back(i, h)

    def move_b(rows, stage, j, h, peer):
        send(cosample.at[h, rows], cosample.at[h, rows], sent.at[4, stage], got_b.at[h, stage, j], peer)

    def begin_b(j, h, p):
        if j == 0:
            add_back(N - 1, h)
        src = rows_of(j * width + (1 - xh) * half_b, half_b)
        send(back.at[h, src], from_xh.at[h, j], sent.at[4, 0], got_b.at[h, 0, j], other_xh)

    def over_b(j, h, p):
        take(half_b, H, got_b.at[h, 0, j])
        a = j * width + xh * half_b
        own = rows_of(a, half_b)
        back[h, own, :] += from_xh[h, j]
        for d in z_order:
            src = rows_of(a + z_at[d] * piece, piece)
            send(back.at[h, src], from_z.at[h, j, d - 1], sent.at[4, 1], got_b.at[h, 1, j], peer_z[d])

    def finish_b(j, h, p):
        own = rows_of(j * width + xh * half_b + z * piece, piece)
        if h == 0:
            totals = []
            for g in range(2):
                take(7 * piece, H, got_b.at[g, 1, j])
                total = back[g, own, :]
                for d in range(1, NZ):
                    total += from_z[g, j, d - 1]
                totals.append(total)
            cosample[0, own, :], cosample[1, own, :] = scale_halves(*totals)
        for d in z_order:
            move_b(own, 2, j, h, peer_z[d])

    def spread_b(j, h, p):
        take(7 * piece, H, got_b.at[h, 2, j])
        move_b(rows_of(j * width + xh * half_b, half_b), 3, j, h, other_xh)

    def use_b(j, h, p):
        take(half_b, H, got_b.at[h, 3, j])
        rows = pl.ds(j * width, width)
        value = cosample[h, rows, :]
        cosample_ref[rows, h * H : (h + 1) * H] = value
        c_terms[h, :, :H], c_terms[h, :, H:] = split(value)
        if j < NB - 1:
            add_last(pl.ds(0, points), j, h)

    sums_2 = [
        tm_sums(
            last.at[h], core_2.at[h], y_2.at[h], x_2.at[h], x2_2.at[h], y2_2.at[h], sent.at[2], sum_2.at[h]
        )
        for h in range(2)
    ]
    gather_ends = tm_gather(refined_ref, sent.at[3], gather_2)

    def begin_2(i, h, p):
        if i % (N // 2) == 0:
            add_last(pl.ds(i * chunk, points // 2), NB - 1, h)
        sums_2[h][0](i)

    def finish_2(i, h, p):
        rows = owned(i, p)
        refined_ref[rows, :H], refined_ref[rows, H:] = scale_halves(sums_2[0][3](i, p), sums_2[1][3](i, p))
        gather_ends[0](i, p)

    stages = [
        [begin_1, lambda i, h, p: over_11(i), lambda i, h, p: over_12(i, p), finish_1]
        + [lambda i, h, p: gathers_1[h][1](i, p), lambda i, h, p: gathers_1[h][2](i, p), use_1],
        [begin_b, over_b, finish_b, spread_b, use_b],
        [begin_2, lambda i, h, p: sums_2[h][1](i), lambda i, h, p: sums_2[h][2](i, p), finish_2]
        + [lambda i, h, p: gather_ends[1](i, p), lambda i, h, p: gather_ends[2](i, p)]
        + [lambda i, h, p: gather_ends[3](i)],
    ]
    for product, stage, at, h, p in ORDER:
        stages[product][stage](at, h, p)

    quarter = 5 * (sub // 4)
    for group, counts in enumerate(
        ([half, quarter, sub // 2], [sub // 2, quarter, half], [half, quarter, sub // 2], [sub // 2, quarter, half])
    ):
        for stage, rows in enumerate(counts):
            take(N * rows, 2 * H, sent.at[group, stage])
    for stage, rows in enumerate((half_b, 7 * piece, 7 * piece, half_b)):
        take(NB * rows, 2 * H, sent.at[4, stage])


def store(refined_ref, cosample_ref, refined_out, cosample_out, sem):
    size = refined_ref.shape[0] // PIECES
    copies = [pltpu.make_async_copy(cosample_ref, cosample_out, sem.at[PIECES])]
    for q in range(PIECES):
        rows = pl.ds(q * size, size)
        copies.append(pltpu.make_async_copy(refined_ref.at[rows], refined_out.at[rows], sem.at[q]))
    for copy in copies:
        copy.start()
    for copy in copies:
        copy.wait()


def local(snapshots, sketch):
    (points, times), k = snapshots.shape, sketch.shape[1]
    chunk, width = points // N, times // NB
    half, sub, half_b = chunk // 2, chunk // 4, width // 2
    vmem = pl.BlockSpec(memory_space=pltpu.VMEM)
    sums = ((N, half), (N, 3, sub // 4), (N, sub // 2), (N, sub // 8), (N, 3, sub // 8))
    sketch = pltpu.with_memory_space_constraint(sketch, pltpu.HBM)
    refined, cosample = pl.pallas_call(
        kernel,
        name="window",
        out_shape=[jax.ShapeDtypeStruct((points, k), F32), jax.ShapeDtypeStruct((times, k), F32)],
        in_specs=[pl.BlockSpec(memory_space=pl.ANY)] * 2,
        out_specs=[vmem, vmem],
        scratch_shapes=[
            pltpu.VMEM((points, times), F32),
            pltpu.VMEM((times, k), F32),
            pltpu.VMEM((points, times), BF16),
            pltpu.VMEM((points, times), BF16),
            pltpu.VMEM((times, k), BF16),
            pltpu.VMEM((times, k), BF16),
            pltpu.VMEM((points, k), F32),
            pltpu.VMEM((2, points, H), F32),
            pltpu.VMEM((2, chunk, 2 * H), BF16),
            pltpu.VMEM((2, times, H), F32),
            pltpu.VMEM((2, times, H), F32),
            pltpu.VMEM((2, width, 2 * H), BF16),
            pltpu.VMEM((2, points, H), F32),
            *[pltpu.VMEM((*shape, k), F32) for shape in sums],
            *[pltpu.VMEM((2, *shape, H), F32) for shape in sums],
            pltpu.VMEM((2, NB, half_b, H), F32),
            pltpu.VMEM((2, NB, NZ - 1, half_b // NZ, H), F32),
            pltpu.SemaphoreType.DMA((points // STEP,)),
            pltpu.SemaphoreType.DMA,
            pltpu.SemaphoreType.DMA((5, 4)),
            pltpu.SemaphoreType.DMA((5, N)),
            pltpu.SemaphoreType.DMA((2, 5, N)),
            pltpu.SemaphoreType.DMA((2, 4, NB)),
            pltpu.SemaphoreType.DMA((2, 5, N)),
            pltpu.SemaphoreType.DMA((5, N)),
        ],
        compiler_params=pltpu.CompilerParams(
            collective_id=0, has_side_effects=True, vmem_limit_bytes=46 << 20
        ),
        cost_estimate=pl.CostEstimate(
            flops=18 * points * times * k, bytes_accessed=4 * points * times, transcendentals=0
        ),
    )(snapshots, sketch)
    hbm = pl.BlockSpec(memory_space=pl.ANY)
    return pl.pallas_call(
        store,
        name="store",
        out_shape=[jax.ShapeDtypeStruct((points, k), F32), jax.ShapeDtypeStruct((times, k), F32)],
        in_specs=[vmem, vmem],
        out_specs=[hbm, hbm],
        scratch_shapes=[pltpu.SemaphoreType.DMA((PIECES + 1,))],
        compiler_params=pltpu.CompilerParams(has_side_effects=True, vmem_limit_bytes=4 << 20),
    )(refined, cosample)


def solution(mesh):
    return jax.shard_map(
        local,
        mesh=mesh,
        in_specs=(P("space", "tm"), P("tm", None)),
        out_specs=(P("space", None), P("tm", None)),
        check_vma=False,
    )
```

```python
import jax
import jax.numpy as jnp
from jax import lax
from jax.experimental import pallas as pl
from jax.experimental.pallas import tpu as pltpu
from jax.sharding import PartitionSpec as P

EPS = 1e-06
MESH = pl.DeviceIdType.MESH
F32, BF16 = jnp.float32, jnp.bfloat16
NZ, NY = 8, 4
H = 128
N = 4
NB = 4
STEP = 256
PIECES = 4
ORDER = [
    (0, 0, 0, 0, 0), (0, 0, 1, 0, 0), (0, 1, 0, 0, 0), (0, 0, 2, 0, 0), (0, 1, 1, 0, 0), (0, 0, 3, 0, 0),
    (0, 1, 2, 0, 0), (0, 2, 0, 0, 1), (0, 2, 0, 0, 0), (0, 1, 3, 0, 0), (0, 2, 1, 0, 0), (0, 2, 1, 0, 1),
    (0, 3, 0, 0, 0), (0, 2, 2, 0, 1), (0, 3, 0, 1, 0), (0, 2, 2, 0, 0), (0, 3, 0, 0, 1), (0, 3, 0, 1, 1),
    (0, 2, 3, 0, 1), (0, 2, 3, 0, 0), (0, 4, 0, 0, 0), (0, 3, 1, 0, 0), (0, 3, 1, 0, 1), (0, 4, 0, 1, 0),
    (0, 3, 2, 0, 0), (0, 3, 2, 1, 0), (0, 3, 1, 1, 0), (0, 3, 2, 0, 1), (0, 4, 0, 0, 1), (0, 3, 1, 1, 1),
    (0, 3, 3, 0, 0), (0, 3, 2, 1, 1), (0, 4, 0, 1, 1), (0, 3, 3, 0, 1), (0, 4, 1, 0, 0), (0, 4, 2, 0, 0),
    (0, 3, 3, 1, 1), (0, 5, 0, 0, 0), (0, 4, 1, 1, 0), (0, 4, 1, 0, 1), (0, 5, 0, 0, 1), (0, 4, 3, 0, 0),
    (0, 4, 2, 1, 0), (0, 5, 0, 1, 0), (0, 4, 2, 0, 1), (0, 3, 3, 1, 0), (0, 5, 0, 1, 1), (0, 4, 2, 1, 1),
    (0, 6, 0, 0, 0), (0, 4, 3, 0, 1), (0, 5, 1, 0, 0), (0, 4, 1, 1, 1), (0, 5, 1, 0, 1), (0, 6, 0, 1, 0),
    (0, 5, 2, 0, 1), (0, 5, 2, 0, 0), (0, 4, 3, 1, 0), (0, 6, 1, 0, 0), (0, 5, 3, 0, 0), (0, 5, 3, 0, 1),
    (0, 4, 3, 1, 1), (0, 5, 1, 1, 0), (0, 6, 2, 0, 0), (0, 5, 1, 1, 1), (0, 6, 3, 0, 0), (1, 0, 0, 0, 0),
    (0, 5, 2, 1, 1), (0, 5, 2, 1, 0), (1, 0, 1, 0, 0), (0, 5, 3, 1, 1), (0, 6, 1, 1, 0), (0, 5, 3, 1, 0),
    (0, 6, 2, 1, 0), (1, 0, 2, 0, 0), (0, 6, 3, 1, 0), (1, 0, 0, 1, 0), (1, 1, 0, 0, 0), (1, 0, 1, 1, 0),
    (1, 1, 1, 0, 0), (1, 0, 2, 1, 0), (1, 0, 3, 0, 0), (1, 1, 2, 0, 0), (1, 0, 3, 1, 0), (1, 1, 0, 1, 0),
    (1, 1, 1, 1, 0), (1, 1, 2, 1, 0), (1, 1, 3, 0, 0), (1, 2, 0, 0, 0), (1, 1, 3, 1, 0), (1, 2, 1, 0, 0),
    (1, 2, 2, 0, 0), (1, 2, 0, 1, 0), (1, 3, 0, 0, 0), (1, 2, 3, 0, 0), (1, 2, 1, 1, 0), (1, 2, 2, 1, 0),
    (1, 3, 1, 0, 0), (1, 3, 2, 0, 0), (1, 4, 0, 0, 0), (1, 3, 0, 1, 0), (1, 2, 3, 1, 0), (1, 3, 3, 0, 0),
    (1, 4, 1, 0, 0), (1, 3, 1, 1, 0), (1, 4, 2, 0, 0), (1, 3, 2, 1, 0), (1, 4, 0, 1, 0), (1, 4, 3, 0, 0),
    (1, 3, 3, 1, 0), (2, 0, 0, 0, 0), (2, 0, 1, 0, 0), (2, 0, 2, 0, 0), (2, 0, 3, 0, 0), (1, 4, 1, 1, 0),
    (2, 1, 0, 0, 0), (1, 4, 2, 1, 0), (2, 1, 3, 0, 0), (2, 1, 1, 0, 0), (1, 4, 3, 1, 0), (2, 0, 0, 1, 0),
    (2, 1, 2, 0, 0), (2, 0, 1, 1, 0), (2, 0, 2, 1, 0), (2, 2, 0, 0, 1), (2, 0, 3, 1, 0), (2, 1, 0, 1, 0),
    (2, 1, 1, 1, 0), (2, 1, 2, 1, 0), (2, 1, 3, 1, 0), (2, 2, 0, 1, 1), (2, 2, 1, 0, 1), (2, 2, 1, 0, 0),
    (2, 2, 0, 0, 0), (2, 2, 0, 1, 0), (2, 2, 1, 1, 1), (2, 2, 2, 0, 1), (2, 2, 2, 1, 1), (2, 2, 2, 0, 0),
    (2, 2, 3, 0, 1), (2, 2, 1, 1, 0), (2, 2, 2, 1, 0), (2, 2, 3, 1, 1), (2, 2, 3, 0, 0), (2, 2, 3, 1, 0),
    (2, 3, 0, 0, 1), (2, 3, 0, 0, 0), (2, 3, 1, 0, 1), (2, 3, 1, 0, 0), (2, 3, 2, 0, 1), (2, 3, 3, 0, 0),
    (2, 3, 3, 0, 1), (2, 3, 2, 0, 0), (2, 4, 0, 0, 0), (2, 4, 0, 0, 1), (2, 4, 1, 0, 0), (2, 4, 3, 0, 0),
    (2, 4, 2, 0, 1), (2, 4, 2, 0, 0), (2, 4, 3, 0, 1), (2, 4, 1, 0, 1), (2, 5, 0, 0, 0), (2, 5, 3, 0, 1),
    (2, 5, 1, 0, 0), (2, 5, 3, 0, 0), (2, 5, 2, 0, 1), (2, 5, 0, 0, 1), (2, 5, 1, 0, 1), (2, 5, 2, 0, 0),
    (2, 6, 3, 0, 0), (2, 6, 0, 0, 0), (2, 6, 1, 0, 0), (2, 6, 2, 0, 0),
]


def split(value):
    high = value.astype(BF16)
    return high, (value - high.astype(F32)).astype(BF16)


def scale_halves(left, right):
    squares = jnp.sum(left * left + right * right, axis=1, keepdims=True)
    factor = lax.rsqrt(squares * (1.0 / (2 * H)) + EPS)
    return left * factor, right * factor


def dot(a, b):
    return jnp.dot(a, b, preferred_element_type=F32)


def dot_t(a, b):
    return lax.dot_general(a, b, (((0,), (0,)), ((), ())), preferred_element_type=F32)


def kernel(
    snap_ref, sketch_ref, refined_ref, cosample_ref,
    wide, sketch, s_hi, s_lo, b_hi, b_lo, part, sample, p_terms, back, cosample, c_terms, last,
    core_1, y_1, x_1, x2_1, y2_1, core_2, y_2, x_2, x2_2, y2_2, from_xh, from_z,
    load_sem, sketch_sem, sent, sum_1, gather_1, got_b, sum_2, gather_2,
):
    points, times = wide.shape
    space, tm = lax.axis_index("space"), lax.axis_index("tm")
    z, xh = space // 2, lax.rem(space, 2)
    xl, y, core = tm // 8, lax.rem(tm // 2, 4), lax.rem(tm, 2)

    def at_tm(xl, y, core):
        return {"space": space, "tm": xl * 8 + y * 2 + core}

    def at_space(z, xh):
        return {"space": z * 2 + xh, "tm": tm}

    other_core, other_x = at_tm(xl, y, 1 - core), at_tm(1 - xl, y, core)
    other_xh = at_space(z, 1 - xh)
    y_at = [lax.rem(y + d, NY) for d in range(NY)]
    z_at = [lax.rem(z + d, NZ) for d in range(NZ)]
    peer_y = [at_tm(xl, y_at[d], core) for d in range(NY)]
    peer_z = [at_space(z_at[d], xh) for d in range(NZ)]
    y_order, z_order = (2, 1, 3), (4, 3, 5, 2, 6, 1, 7)

    chunk, width = points // N, times // NB
    half, sub = chunk // 2, chunk // 4
    half_b = width // 2
    piece = half_b // NZ

    def load(q):
        rows = pl.ds(q * STEP, STEP)
        return pltpu.make_async_copy(snap_ref.at[rows], wide.at[rows], load_sem.at[q])

    load_sketch = pltpu.make_async_copy(sketch_ref, sketch, sketch_sem)
    load_sketch.start()
    load(0).start()

    barrier = pltpu.get_barrier_semaphore()
    peers = [other_core, other_x, other_xh, *peer_y[1:], *peer_z[1:]]
    for peer in peers:
        pl.semaphore_signal(barrier, inc=1, device_id=peer, device_id_type=MESH)


    def send(src, dst, sent, arrived, peer):
        pltpu.make_async_remote_copy(
            src_ref=src, dst_ref=dst, send_sem=sent, recv_sem=arrived, device_id=peer, device_id_type=MESH
        ).start()

    def take(rows, columns, sem):
        ref = part.at[pl.ds(0, rows * columns // (2 * H))]
        pltpu.make_async_copy(ref, ref, sem).wait()

    def rows_of(start, size):
        return pl.ds(pl.multiple_of(start, 8), size)

    def mine(i):
        return i * chunk + core * half

    def tm_sums(summed, from_core, from_y, from_x, from_x2, from_y2, sent, got):
        columns = summed.shape[1]

        def first(i):
            src = rows_of(i * chunk + (1 - core) * half, half)
            send(summed.at[src], from_core.at[i], sent.at[0], got.at[0, i], other_core)

        def over_1(i):
            take(half, columns, got.at[0, i])
            a, b = mine(i), mine(i) + sub
            own = rows_of(a, half)
            summed[own, :] += from_core[i]
            for d in y_order:
                src = rows_of(a + y_at[d] * (sub // 4), sub // 4)
                send(summed.at[src], from_y.at[i, d - 1], sent.at[1], got.at[1, i], peer_y[d])
            src = rows_of(b + (1 - xl) * (sub // 2), sub // 2)
            send(summed.at[src], from_x.at[i], sent.at[1], got.at[2, i], other_x)

        def over_2(i, p):
            if p == 0:
                take(3 * (sub // 4), columns, got.at[1, i])
                a = mine(i) + y * (sub // 4)
                own = rows_of(a, sub // 4)
                summed[own, :] += from_y[i, 0] + from_y[i, 1] + from_y[i, 2]
                src = rows_of(a + (1 - xl) * (sub // 8), sub // 8)
                send(summed.at[src], from_x2.at[i], sent.at[2], got.at[3, i], other_x)
            else:
                take(sub // 2, columns, got.at[2, i])
                b = mine(i) + sub + xl * (sub // 2)
                own = rows_of(b, sub // 2)
                summed[own, :] += from_x[i]
                for d in y_order:
                    src = rows_of(b + y_at[d] * (sub // 8), sub // 8)
                    send(summed.at[src], from_y2.at[i, d - 1], sent.at[2], got.at[4, i], peer_y[d])

        def total(i, p):
            own = owned(i, p)
            if p == 0:
                take(sub // 8, columns, got.at[3, i])
                return summed[own, :] + from_x2[i]
            take(3 * (sub // 8), columns, got.at[4, i])
            return summed[own, :] + (from_y2[i, 0] + from_y2[i, 1] + from_y2[i, 2])

        return first, over_1, over_2, total

    def owned(i, p):
        if p == 0:
            return rows_of(mine(i) + y * (sub // 4) + xl * (sub // 8), sub // 8)
        return rows_of(mine(i) + sub + xl * (sub // 2) + y * (sub // 8), sub // 8)

    def tm_gather(gathered, sent, got):
        columns = gathered.shape[1]

        def move(rows, stage, place, i, peer):
            send(gathered.at[rows], gathered.at[rows], sent.at[stage], got.at[place, i], peer)

        def start(i, p):
            own = owned(i, p)
            if p == 0:
                move(own, 0, 0, i, other_x)
            else:
                for d in y_order:
                    move(own, 0, 1, i, peer_y[d])

        def spread(i, p):
            if p == 0:
                take(sub // 8, columns, got.at[0, i])
                rows = rows_of(mine(i) + y * (sub // 4), sub // 4)
                for d in y_order:
                    move(rows, 1, 2, i, peer_y[d])
            else:
                take(3 * (sub // 8), columns, got.at[1, i])
                move(rows_of(mine(i) + sub + xl * (sub // 2), sub // 2), 1, 3, i, other_x)

        def to_core(i, p):
            if p == 0:
                take(3 * (sub // 4), columns, got.at[2, i])
            else:
                take(sub // 2, columns, got.at[3, i])
            move(rows_of(mine(i) + p * sub, sub), 2, 4, i, other_core)

        def arrive(i):
            take(half, columns, got.at[4, i])

        return start, spread, to_core, arrive

    def multiply_1(i):
        size = STEP if i == 0 else chunk
        for start in range(i * chunk, (i + 1) * chunk, size):
            for q in range(start // STEP, (start + size) // STEP):
                load(q).wait()
                if q == 0:
                    for later in range(2 * chunk // STEP, points // STEP):
                        load(later).start()
            rows = pl.ds(start, size)
            high, low = split(wide[rows, :])
            s_hi[rows, :] = high
            s_lo[rows, :] = low
            part[rows, :] = dot(high, b_hi[...]) + (dot(high, b_lo[...]) + dot(low, b_hi[...]))

    def add_back(i, h):
        rows = pl.ds(i * chunk, chunk)
        terms = p_terms[h]
        value = dot_t(s_hi[rows, :], terms) + dot_t(s_lo[rows, :], terms)
        value = value[:, :H] + value[:, H:]
        back[h] = value if i == 0 else back[h] + value

    def add_last(rows, j, h):
        columns = pl.ds(j * width, width)
        terms = c_terms[h]
        value = dot(s_hi[rows, columns], terms) + dot(s_lo[rows, columns], terms)
        value = value[:, :H] + value[:, H:]
        last[h, rows, :] = value if j == 0 else last[h, rows, :] + value

    first_1, over_11, over_12, total_1 = tm_sums(part, core_1, y_1, x_1, x2_1, y2_1, sent.at[0], sum_1)
    gathers_1 = [tm_gather(sample.at[h], sent.at[1], gather_1.at[h]) for h in range(2)]

    def begin_1(i, h, p):
        if i == 0:
            load_sketch.wait()
            for q in range(1, 2 * chunk // STEP):
                load(q).start()
            b_hi[...], b_lo[...] = split(sketch[...])
        multiply_1(i)
        if i == 0:
            pl.semaphore_wait(barrier, len(peers))
        first_1(i)

    def finish_1(i, h, p):
        if h == 0:
            rows, value = owned(i, p), total_1(i, p)
            sample[0, rows, :], sample[1, rows, :] = scale_halves(value[:, :H], value[:, H:])
        gathers_1[h][0](i, p)

    def use_1(i, h, p):
        gathers_1[h][3](i)
        rows = pl.ds(i * chunk, chunk)
        p_terms[h, :, :H], p_terms[h, :, H:] = split(sample[h, rows, :])
        if i < N - 1:
            add_back(i, h)

    def move_b(rows, stage, j, h, peer):
        send(cosample.at[h, rows], cosample.at[h, rows], sent.at[4, stage], got_b.at[h, stage, j], peer)

    def begin_b(j, h, p):
        if j == 0:
            add_back(N - 1, h)
        src = rows_of(j * width + (1 - xh) * half_b, half_b)
        send(back.at[h, src], from_xh.at[h, j], sent.at[4, 0], got_b.at[h, 0, j], other_xh)

    def over_b(j, h, p):
        take(half_b, H, got_b.at[h, 0, j])
        a = j * width + xh * half_b
        own = rows_of(a, half_b)
        back[h, own, :] += from_xh[h, j]
        for d in z_order:
            src = rows_of(a + z_at[d] * piece, piece)
            send(back.at[h, src], from_z.at[h, j, d - 1], sent.at[4, 1], got_b.at[h, 1, j], peer_z[d])

    def finish_b(j, h, p):
        own = rows_of(j * width + xh * half_b + z * piece, piece)
        if h == 0:
            totals = []
            for g in range(2):
                take(7 * piece, H, got_b.at[g, 1, j])
                total = back[g, own, :]
                for d in range(1, NZ):
                    total += from_z[g, j, d - 1]
                totals.append(total)
            cosample[0, own, :], cosample[1, own, :] = scale_halves(*totals)
        for d in z_order:
            move_b(own, 2, j, h, peer_z[d])

    def spread_b(j, h, p):
        take(7 * piece, H, got_b.at[h, 2, j])
        move_b(rows_of(j * width + xh * half_b, half_b), 3, j, h, other_xh)

    def use_b(j, h, p):
        take(half_b, H, got_b.at[h, 3, j])
        rows = pl.ds(j * width, width)
        value = cosample[h, rows, :]
        cosample_ref[rows, h * H : (h + 1) * H] = value
        c_terms[h, :, :H], c_terms[h, :, H:] = split(value)
        if j < NB - 1:
            add_last(pl.ds(0, points), j, h)

    sums_2 = [
        tm_sums(
            last.at[h], core_2.at[h], y_2.at[h], x_2.at[h], x2_2.at[h], y2_2.at[h], sent.at[2], sum_2.at[h]
        )
        for h in range(2)
    ]
    gather_ends = tm_gather(refined_ref, sent.at[3], gather_2)

    def begin_2(i, h, p):
        if i % (N // 2) == 0:
            add_last(pl.ds(i * chunk, points // 2), NB - 1, h)
        sums_2[h][0](i)

    def finish_2(i, h, p):
        rows = owned(i, p)
        refined_ref[rows, :H], refined_ref[rows, H:] = scale_halves(sums_2[0][3](i, p), sums_2[1][3](i, p))
        gather_ends[0](i, p)

    stages = [
        [begin_1, lambda i, h, p: over_11(i), lambda i, h, p: over_12(i, p), finish_1]
        + [lambda i, h, p: gathers_1[h][1](i, p), lambda i, h, p: gathers_1[h][2](i, p), use_1],
        [begin_b, over_b, finish_b, spread_b, use_b],
        [begin_2, lambda i, h, p: sums_2[h][1](i), lambda i, h, p: sums_2[h][2](i, p), finish_2]
        + [lambda i, h, p: gather_ends[1](i, p), lambda i, h, p: gather_ends[2](i, p)]
        + [lambda i, h, p: gather_ends[3](i)],
    ]
    for product, stage, at, h, p in ORDER:
        stages[product][stage](at, h, p)

    quarter = 5 * (sub // 4)
    for group, counts in enumerate(
        ([half, quarter, sub // 2], [sub // 2, quarter, half], [half, quarter, sub // 2], [sub // 2, quarter, half])
    ):
        for stage, rows in enumerate(counts):
            take(N * rows, 2 * H, sent.at[group, stage])
    for stage, rows in enumerate((half_b, 7 * piece, 7 * piece, half_b)):
        take(NB * rows, 2 * H, sent.at[4, stage])


def store(refined_ref, cosample_ref, refined_out, cosample_out, sem):
    size = refined_ref.shape[0] // PIECES
    copies = [pltpu.make_async_copy(cosample_ref, cosample_out, sem.at[PIECES])]
    for q in range(PIECES):
        rows = pl.ds(q * size, size)
        copies.append(pltpu.make_async_copy(refined_ref.at[rows], refined_out.at[rows], sem.at[q]))
    for copy in copies:
        copy.start()
    for copy in copies:
        copy.wait()


def local(snapshots, sketch):
    (points, times), k = snapshots.shape, sketch.shape[1]
    chunk, width = points // N, times // NB
    half, sub, half_b = chunk // 2, chunk // 4, width // 2
    vmem = pl.BlockSpec(memory_space=pltpu.VMEM)
    sums = ((N, half), (N, 3, sub // 4), (N, sub // 2), (N, sub // 8), (N, 3, sub // 8))
    sketch = pltpu.with_memory_space_constraint(sketch, pltpu.HBM)
    refined, cosample = pl.pallas_call(
        kernel,
        name="window",
        out_shape=[jax.ShapeDtypeStruct((points, k), F32), jax.ShapeDtypeStruct((times, k), F32)],
        in_specs=[pl.BlockSpec(memory_space=pl.ANY)] * 2,
        out_specs=[vmem, vmem],
        scratch_shapes=[
            pltpu.VMEM((points, times), F32),
            pltpu.VMEM((times, k), F32),
            pltpu.VMEM((points, times), BF16),
            pltpu.VMEM((points, times), BF16),
            pltpu.VMEM((times, k), BF16),
            pltpu.VMEM((times, k), BF16),
            pltpu.VMEM((points, k), F32),
            pltpu.VMEM((2, points, H), F32),
            pltpu.VMEM((2, chunk, 2 * H), BF16),
            pltpu.VMEM((2, times, H), F32),
            pltpu.VMEM((2, times, H), F32),
            pltpu.VMEM((2, width, 2 * H), BF16),
            pltpu.VMEM((2, points, H), F32),
            *[pltpu.VMEM((*shape, k), F32) for shape in sums],
            *[pltpu.VMEM((2, *shape, H), F32) for shape in sums],
            pltpu.VMEM((2, NB, half_b, H), F32),
            pltpu.VMEM((2, NB, NZ - 1, half_b // NZ, H), F32),
            pltpu.SemaphoreType.DMA((points // STEP,)),
            pltpu.SemaphoreType.DMA,
            pltpu.SemaphoreType.DMA((5, 4)),
            pltpu.SemaphoreType.DMA((5, N)),
            pltpu.SemaphoreType.DMA((2, 5, N)),
            pltpu.SemaphoreType.DMA((2, 4, NB)),
            pltpu.SemaphoreType.DMA((2, 5, N)),
            pltpu.SemaphoreType.DMA((5, N)),
        ],
        compiler_params=pltpu.CompilerParams(
            collective_id=0, has_side_effects=True, vmem_limit_bytes=46 << 20
        ),
        cost_estimate=pl.CostEstimate(
            flops=18 * points * times * k, bytes_accessed=4 * points * times, transcendentals=0
        ),
    )(snapshots, sketch)
    hbm = pl.BlockSpec(memory_space=pl.ANY)
    return pl.pallas_call(
        store,
        name="store",
        out_shape=[jax.ShapeDtypeStruct((points, k), F32), jax.ShapeDtypeStruct((times, k), F32)],
        in_specs=[vmem, vmem],
        out_specs=[hbm, hbm],
        scratch_shapes=[pltpu.SemaphoreType.DMA((PIECES + 1,))],
        compiler_params=pltpu.CompilerParams(has_side_effects=True, vmem_limit_bytes=4 << 20),
    )(refined, cosample)


def solution(mesh):
    return jax.shard_map(
        local,
        mesh=mesh,
        in_specs=(P("space", "tm"), P("tm", None)),
        out_specs=(P("space", None), P("tm", None)),
        check_vma=False,
    )
```

```python
import jax
import jax.numpy as jnp
from jax import lax
from jax.experimental import pallas as pl
from jax.experimental.pallas import tpu as pltpu
from jax.sharding import PartitionSpec as P

EPS = 1e-06
MESH = pl.DeviceIdType.MESH
F32, BF16 = jnp.float32, jnp.bfloat16
NZ, NY = 8, 4
H = 128
N = 4
NB = 4
STEP = 256
PIECES = 4
ORDER = [
    (0, 0, 0, 0, 0), (0, 0, 1, 0, 0), (0, 1, 0, 0, 0), (0, 0, 2, 0, 0), (0, 1, 1, 0, 0), (0, 0, 3, 0, 0),
    (0, 1, 2, 0, 0), (0, 2, 0, 0, 1), (0, 2, 0, 0, 0), (0, 1, 3, 0, 0), (0, 2, 1, 0, 0), (0, 2, 1, 0, 1),
    (0, 3, 0, 0, 0), (0, 2, 2, 0, 1), (0, 3, 0, 1, 0), (0, 2, 2, 0, 0), (0, 3, 0, 0, 1), (0, 3, 0, 1, 1),
    (0, 2, 3, 0, 1), (0, 2, 3, 0, 0), (0, 4, 0, 0, 0), (0, 3, 1, 0, 0), (0, 3, 1, 0, 1), (0, 4, 0, 1, 0),
    (0, 3, 2, 0, 0), (0, 3, 2, 1, 0), (0, 3, 1, 1, 0), (0, 3, 2, 0, 1), (0, 4, 0, 0, 1), (0, 3, 1, 1, 1),
    (0, 3, 3, 0, 0), (0, 3, 2, 1, 1), (0, 4, 0, 1, 1), (0, 3, 3, 0, 1), (0, 4, 1, 0, 0), (0, 4, 2, 0, 0),
    (0, 3, 3, 1, 1), (0, 5, 0, 0, 0), (0, 4, 1, 1, 0), (0, 4, 1, 0, 1), (0, 5, 0, 0, 1), (0, 4, 3, 0, 0),
    (0, 4, 2, 1, 0), (0, 5, 0, 1, 0), (0, 4, 2, 0, 1), (0, 3, 3, 1, 0), (0, 5, 0, 1, 1), (0, 4, 2, 1, 1),
    (0, 6, 0, 0, 0), (0, 4, 3, 0, 1), (0, 5, 1, 0, 0), (0, 4, 1, 1, 1), (0, 5, 1, 0, 1), (0, 6, 0, 1, 0),
    (0, 5, 2, 0, 1), (0, 5, 2, 0, 0), (0, 4, 3, 1, 0), (0, 6, 1, 0, 0), (0, 5, 3, 0, 0), (0, 5, 3, 0, 1),
    (0, 4, 3, 1, 1), (0, 5, 1, 1, 0), (0, 6, 2, 0, 0), (0, 5, 1, 1, 1), (0, 6, 3, 0, 0), (1, 0, 0, 0, 0),
    (0, 5, 2, 1, 1), (0, 5, 2, 1, 0), (1, 0, 1, 0, 0), (0, 5, 3, 1, 1), (0, 6, 1, 1, 0), (0, 5, 3, 1, 0),
    (0, 6, 2, 1, 0), (1, 0, 2, 0, 0), (0, 6, 3, 1, 0), (1, 0, 0, 1, 0), (1, 1, 0, 0, 0), (1, 0, 1, 1, 0),
    (1, 1, 1, 0, 0), (1, 0, 2, 1, 0), (1, 0, 3, 0, 0), (1, 1, 2, 0, 0), (1, 0, 3, 1, 0), (1, 1, 0, 1, 0),
    (1, 1, 1, 1, 0), (1, 1, 2, 1, 0), (1, 1, 3, 0, 0), (1, 2, 0, 0, 0), (1, 1, 3, 1, 0), (1, 2, 1, 0, 0),
    (1, 2, 2, 0, 0), (1, 2, 0, 1, 0), (1, 3, 0, 0, 0), (1, 2, 3, 0, 0), (1, 2, 1, 1, 0), (1, 2, 2, 1, 0),
    (1, 3, 1, 0, 0), (1, 3, 2, 0, 0), (1, 4, 0, 0, 0), (1, 3, 0, 1, 0), (1, 2, 3, 1, 0), (1, 3, 3, 0, 0),
    (1, 4, 1, 0, 0), (1, 3, 1, 1, 0), (1, 4, 2, 0, 0), (1, 3, 2, 1, 0), (1, 4, 0, 1, 0), (1, 4, 3, 0, 0),
    (1, 3, 3, 1, 0), (2, 0, 0, 0, 0), (2, 0, 1, 0, 0), (2, 0, 2, 0, 0), (2, 0, 3, 0, 0), (1, 4, 1, 1, 0),
    (2, 1, 0, 0, 0), (1, 4, 2, 1, 0), (2, 1, 3, 0, 0), (2, 1, 1, 0, 0), (1, 4, 3, 1, 0), (2, 0, 0, 1, 0),
    (2, 1, 2, 0, 0), (2, 0, 1, 1, 0), (2, 0, 2, 1, 0), (2, 2, 0, 0, 1), (2, 0, 3, 1, 0), (2, 1, 0, 1, 0),
    (2, 1, 1, 1, 0), (2, 1, 2, 1, 0), (2, 1, 3, 1, 0), (2, 2, 0, 1, 1), (2, 2, 1, 0, 1), (2, 2, 1, 0, 0),
    (2, 2, 0, 0, 0), (2, 2, 0, 1, 0), (2, 2, 1, 1, 1), (2, 2, 2, 0, 1), (2, 2, 2, 1, 1), (2, 2, 2, 0, 0),
    (2, 2, 3, 0, 1), (2, 2, 1, 1, 0), (2, 2, 2, 1, 0), (2, 2, 3, 1, 1), (2, 2, 3, 0, 0), (2, 2, 3, 1, 0),
    (2, 3, 0, 0, 1), (2, 3, 0, 0, 0), (2, 3, 1, 0, 1), (2, 3, 1, 0, 0), (2, 3, 2, 0, 1), (2, 3, 3, 0, 0),
    (2, 3, 3, 0, 1), (2, 3, 2, 0, 0), (2, 4, 0, 0, 0), (2, 4, 0, 0, 1), (2, 4, 1, 0, 0), (2, 4, 3, 0, 0),
    (2, 4, 2, 0, 1), (2, 4, 2, 0, 0), (2, 4, 3, 0, 1), (2, 4, 1, 0, 1), (2, 5, 0, 0, 0), (2, 5, 3, 0, 1),
    (2, 5, 1, 0, 0), (2, 5, 3, 0, 0), (2, 5, 2, 0, 1), (2, 5, 0, 0, 1), (2, 5, 1, 0, 1), (2, 5, 2, 0, 0),
    (2, 6, 3, 0, 0), (2, 6, 0, 0, 0), (2, 6, 1, 0, 0), (2, 6, 2, 0, 0),
]


def split(value):
    high = value.astype(BF16)
    return high, (value - high.astype(F32)).astype(BF16)


def scale_halves(left, right):
    squares = jnp.sum(left * left + right * right, axis=1, keepdims=True)
    factor = lax.rsqrt(squares * (1.0 / (2 * H)) + EPS)
    return left * factor, right * factor


def dot(a, b):
    return jnp.dot(a, b, preferred_element_type=F32)


def dot_t(a, b):
    return lax.dot_general(a, b, (((0,), (0,)), ((), ())), preferred_element_type=F32)


def kernel(
    snap_ref, sketch_ref, refined_ref, cosample_ref,
    wide, sketch, s_hi, s_lo, b_hi, b_lo, part, sample, p_terms, back, cosample, c_terms, last,
    core_1, y_1, x_1, x2_1, y2_1, core_2, y_2, x_2, x2_2, y2_2, from_xh, from_z,
    load_sem, sketch_sem, sent, sum_1, gather_1, got_b, sum_2, gather_2,
):
    points, times = wide.shape
    space, tm = lax.axis_index("space"), lax.axis_index("tm")
    z, xh = space // 2, lax.rem(space, 2)
    xl, y, core = tm // 8, lax.rem(tm // 2, 4), lax.rem(tm, 2)

    def at_tm(xl, y, core):
        return {"space": space, "tm": xl * 8 + y * 2 + core}

    def at_space(z, xh):
        return {"space": z * 2 + xh, "tm": tm}

    other_core, other_x = at_tm(xl, y, 1 - core), at_tm(1 - xl, y, core)
    other_xh = at_space(z, 1 - xh)
    y_at = [lax.rem(y + d, NY) for d in range(NY)]
    z_at = [lax.rem(z + d, NZ) for d in range(NZ)]
    peer_y = [at_tm(xl, y_at[d], core) for d in range(NY)]
    peer_z = [at_space(z_at[d], xh) for d in range(NZ)]
    y_order, z_order = (2, 1, 3), (4, 3, 5, 2, 6, 1, 7)

    chunk, width = points // N, times // NB
    half, sub = chunk // 2, chunk // 4
    half_b = width // 2
    piece = half_b // NZ

    def load(q):
        start = q * STEP
        if q < 2:
            start = pl.multiple_of((1 - core if q == 0 else core) * STEP, STEP)
        rows = pl.ds(start, STEP)
        return pltpu.make_async_copy(snap_ref.at[rows], wide.at[rows], load_sem.at[q])

    load_sketch = pltpu.make_async_copy(sketch_ref, sketch, sketch_sem)
    load_sketch.start()
    load(0).start()

    barrier = pltpu.get_barrier_semaphore()
    peers = [other_core, other_x, other_xh, *peer_y[1:], *peer_z[1:]]
    for peer in peers:
        pl.semaphore_signal(barrier, inc=1, device_id=peer, device_id_type=MESH)


    def send(src, dst, sent, arrived, peer):
        pltpu.make_async_remote_copy(
            src_ref=src, dst_ref=dst, send_sem=sent, recv_sem=arrived, device_id=peer, device_id_type=MESH
        ).start()

    def take(rows, columns, sem):
        ref = part.at[pl.ds(0, rows * columns // (2 * H))]
        pltpu.make_async_copy(ref, ref, sem).wait()

    def rows_of(start, size):
        return pl.ds(pl.multiple_of(start, 8), size)

    def mine(i):
        return i * chunk + core * half

    def tm_sums(summed, from_core, from_y, from_x, from_x2, from_y2, sent, got):
        columns = summed.shape[1]

        def first(i):
            src = rows_of(i * chunk + (1 - core) * half, half)
            send(summed.at[src], from_core.at[i], sent.at[0], got.at[0, i], other_core)

        def over_1(i):
            take(half, columns, got.at[0, i])
            a, b = mine(i), mine(i) + sub
            own = rows_of(a, half)
            summed[own, :] += from_core[i]
            for d in y_order:
                src = rows_of(a + y_at[d] * (sub // 4), sub // 4)
                send(summed.at[src], from_y.at[i, d - 1], sent.at[1], got.at[1, i], peer_y[d])
            src = rows_of(b + (1 - xl) * (sub // 2), sub // 2)
            send(summed.at[src], from_x.at[i], sent.at[1], got.at[2, i], other_x)

        def over_2(i, p):
            if p == 0:
                take(3 * (sub // 4), columns, got.at[1, i])
                a = mine(i) + y * (sub // 4)
                own = rows_of(a, sub // 4)
                summed[own, :] += from_y[i, 0] + from_y[i, 1] + from_y[i, 2]
                src = rows_of(a + (1 - xl) * (sub // 8), sub // 8)
                send(summed.at[src], from_x2.at[i], sent.at[2], got.at[3, i], other_x)
            else:
                take(sub // 2, columns, got.at[2, i])
                b = mine(i) + sub + xl * (sub // 2)
                own = rows_of(b, sub // 2)
                summed[own, :] += from_x[i]
                for d in y_order:
                    src = rows_of(b + y_at[d] * (sub // 8), sub // 8)
                    send(summed.at[src], from_y2.at[i, d - 1], sent.at[2], got.at[4, i], peer_y[d])

        def total(i, p):
            own = owned(i, p)
            if p == 0:
                take(sub // 8, columns, got.at[3, i])
                return summed[own, :] + from_x2[i]
            take(3 * (sub // 8), columns, got.at[4, i])
            return summed[own, :] + (from_y2[i, 0] + from_y2[i, 1] + from_y2[i, 2])

        return first, over_1, over_2, total

    def owned(i, p):
        if p == 0:
            return rows_of(mine(i) + y * (sub // 4) + xl * (sub // 8), sub // 8)
        return rows_of(mine(i) + sub + xl * (sub // 2) + y * (sub // 8), sub // 8)

    def tm_gather(gathered, sent, got):
        columns = gathered.shape[1]

        def move(rows, stage, place, i, peer):
            send(gathered.at[rows], gathered.at[rows], sent.at[stage], got.at[place, i], peer)

        def start(i, p):
            own = owned(i, p)
            if p == 0:
                move(own, 0, 0, i, other_x)
            else:
                for d in y_order:
                    move(own, 0, 1, i, peer_y[d])

        def spread(i, p):
            if p == 0:
                take(sub // 8, columns, got.at[0, i])
                rows = rows_of(mine(i) + y * (sub // 4), sub // 4)
                for d in y_order:
                    move(rows, 1, 2, i, peer_y[d])
            else:
                take(3 * (sub // 8), columns, got.at[1, i])
                move(rows_of(mine(i) + sub + xl * (sub // 2), sub // 2), 1, 3, i, other_x)

        def to_core(i, p):
            if p == 0:
                take(3 * (sub // 4), columns, got.at[2, i])
            else:
                take(sub // 2, columns, got.at[3, i])
            move(rows_of(mine(i) + p * sub, sub), 2, 4, i, other_core)

        def arrive(i):
            take(half, columns, got.at[4, i])

        return start, spread, to_core, arrive

    def multiply_1(rows):
        high, low = split(wide[rows, :])
        s_hi[rows, :] = high
        s_lo[rows, :] = low
        part[rows, :] = dot(high, b_hi[...]) + (dot(high, b_lo[...]) + dot(low, b_hi[...]))

    def add_back(i, h):
        rows = pl.ds(i * chunk, chunk)
        terms = p_terms[h]
        value = dot_t(s_hi[rows, :], terms) + dot_t(s_lo[rows, :], terms)
        value = value[:, :H] + value[:, H:]
        back[h] = value if i == 0 else back[h] + value

    def add_last(rows, j, h):
        columns = pl.ds(j * width, width)
        terms = c_terms[h]
        value = dot(s_hi[rows, columns], terms) + dot(s_lo[rows, columns], terms)
        value = value[:, :H] + value[:, H:]
        last[h, rows, :] = value if j == 0 else last[h, rows, :] + value

    first_1, over_11, over_12, total_1 = tm_sums(part, core_1, y_1, x_1, x2_1, y2_1, sent.at[0], sum_1)
    gathers_1 = [tm_gather(sample.at[h], sent.at[1], gather_1.at[h]) for h in range(2)]

    def begin_1(i, h, p):
        if i == 0:
            load_sketch.wait()
            for q in range(1, 2 * chunk // STEP):
                load(q).start()
            b_hi[...], b_lo[...] = split(sketch[...])
            load(0).wait()
            for q in range(2 * chunk // STEP, points // STEP):
                load(q).start()
            multiply_1(pl.ds(pl.multiple_of((1 - core) * STEP, STEP), STEP))
            pl.semaphore_wait(barrier, len(peers))
            first_1(i)
            load(1).wait()
            multiply_1(pl.ds(pl.multiple_of(core * STEP, STEP), STEP))
        else:
            for q in range(i * chunk // STEP, (i + 1) * chunk // STEP):
                load(q).wait()
            multiply_1(pl.ds(i * chunk, chunk))
            first_1(i)

    def finish_1(i, h, p):
        if h == 0:
            rows, value = owned(i, p), total_1(i, p)
            sample[0, rows, :], sample[1, rows, :] = scale_halves(value[:, :H], value[:, H:])
        gathers_1[h][0](i, p)

    def use_1(i, h, p):
        gathers_1[h][3](i)
        rows = pl.ds(i * chunk, chunk)
        p_terms[h, :, :H], p_terms[h, :, H:] = split(sample[h, rows, :])
        if i < N - 1:
            add_back(i, h)

    def move_b(rows, stage, j, h, peer):
        send(cosample.at[h, rows], cosample.at[h, rows], sent.at[4, stage], got_b.at[h, stage, j], peer)

    def begin_b(j, h, p):
        if j == 0:
            add_back(N - 1, h)
        src = rows_of(j * width + (1 - xh) * half_b, half_b)
        send(back.at[h, src], from_xh.at[h, j], sent.at[4, 0], got_b.at[h, 0, j], other_xh)

    def over_b(j, h, p):
        take(half_b, H, got_b.at[h, 0, j])
        a = j * width + xh * half_b
        own = rows_of(a, half_b)
        back[h, own, :] += from_xh[h, j]
        for d in z_order:
            src = rows_of(a + z_at[d] * piece, piece)
            send(back.at[h, src], from_z.at[h, j, d - 1], sent.at[4, 1], got_b.at[h, 1, j], peer_z[d])

    def finish_b(j, h, p):
        own = rows_of(j * width + xh * half_b + z * piece, piece)
        if h == 0:
            totals = []
            for g in range(2):
                take(7 * piece, H, got_b.at[g, 1, j])
                total = back[g, own, :]
                for d in range(1, NZ):
                    total += from_z[g, j, d - 1]
                totals.append(total)
            cosample[0, own, :], cosample[1, own, :] = scale_halves(*totals)
        for d in z_order:
            move_b(own, 2, j, h, peer_z[d])

    def spread_b(j, h, p):
        take(7 * piece, H, got_b.at[h, 2, j])
        move_b(rows_of(j * width + xh * half_b, half_b), 3, j, h, other_xh)

    def use_b(j, h, p):
        take(half_b, H, got_b.at[h, 3, j])
        rows = pl.ds(j * width, width)
        value = cosample[h, rows, :]
        cosample_ref[rows, h * H : (h + 1) * H] = value
        c_terms[h, :, :H], c_terms[h, :, H:] = split(value)
        if j < NB - 1:
            add_last(pl.ds(0, points), j, h)

    sums_2 = [
        tm_sums(
            last.at[h], core_2.at[h], y_2.at[h], x_2.at[h], x2_2.at[h], y2_2.at[h], sent.at[2], sum_2.at[h]
        )
        for h in range(2)
    ]
    gather_ends = tm_gather(refined_ref, sent.at[3], gather_2)

    def begin_2(i, h, p):
        if i % (N // 2) == 0:
            add_last(pl.ds(i * chunk, points // 2), NB - 1, h)
        sums_2[h][0](i)

    def finish_2(i, h, p):
        rows = owned(i, p)
        refined_ref[rows, :H], refined_ref[rows, H:] = scale_halves(sums_2[0][3](i, p), sums_2[1][3](i, p))
        gather_ends[0](i, p)

    stages = [
        [begin_1, lambda i, h, p: over_11(i), lambda i, h, p: over_12(i, p), finish_1]
        + [lambda i, h, p: gathers_1[h][1](i, p), lambda i, h, p: gathers_1[h][2](i, p), use_1],
        [begin_b, over_b, finish_b, spread_b, use_b],
        [begin_2, lambda i, h, p: sums_2[h][1](i), lambda i, h, p: sums_2[h][2](i, p), finish_2]
        + [lambda i, h, p: gather_ends[1](i, p), lambda i, h, p: gather_ends[2](i, p)]
        + [lambda i, h, p: gather_ends[3](i)],
    ]
    for product, stage, at, h, p in ORDER:
        stages[product][stage](at, h, p)

    quarter = 5 * (sub // 4)
    for group, counts in enumerate(
        ([half, quarter, sub // 2], [sub // 2, quarter, half], [half, quarter, sub // 2], [sub // 2, quarter, half])
    ):
        for stage, rows in enumerate(counts):
            take(N * rows, 2 * H, sent.at[group, stage])
    for stage, rows in enumerate((half_b, 7 * piece, 7 * piece, half_b)):
        take(NB * rows, 2 * H, sent.at[4, stage])


def store(refined_ref, cosample_ref, refined_out, cosample_out, sem):
    size = refined_ref.shape[0] // PIECES
    copies = [pltpu.make_async_copy(cosample_ref, cosample_out, sem.at[PIECES])]
    for q in range(PIECES):
        rows = pl.ds(q * size, size)
        copies.append(pltpu.make_async_copy(refined_ref.at[rows], refined_out.at[rows], sem.at[q]))
    for copy in copies:
        copy.start()
    for copy in copies:
        copy.wait()


def local(snapshots, sketch):
    (points, times), k = snapshots.shape, sketch.shape[1]
    chunk, width = points // N, times // NB
    half, sub, half_b = chunk // 2, chunk // 4, width // 2
    vmem = pl.BlockSpec(memory_space=pltpu.VMEM)
    sums = ((N, half), (N, 3, sub // 4), (N, sub // 2), (N, sub // 8), (N, 3, sub // 8))
    sketch = pltpu.with_memory_space_constraint(sketch, pltpu.HBM)
    refined, cosample = pl.pallas_call(
        kernel,
        name="window",
        out_shape=[jax.ShapeDtypeStruct((points, k), F32), jax.ShapeDtypeStruct((times, k), F32)],
        in_specs=[pl.BlockSpec(memory_space=pl.ANY)] * 2,
        out_specs=[vmem, vmem],
        scratch_shapes=[
            pltpu.VMEM((points, times), F32),
            pltpu.VMEM((times, k), F32),
            pltpu.VMEM((points, times), BF16),
            pltpu.VMEM((points, times), BF16),
            pltpu.VMEM((times, k), BF16),
            pltpu.VMEM((times, k), BF16),
            pltpu.VMEM((points, k), F32),
            pltpu.VMEM((2, points, H), F32),
            pltpu.VMEM((2, chunk, 2 * H), BF16),
            pltpu.VMEM((2, times, H), F32),
            pltpu.VMEM((2, times, H), F32),
            pltpu.VMEM((2, width, 2 * H), BF16),
            pltpu.VMEM((2, points, H), F32),
            *[pltpu.VMEM((*shape, k), F32) for shape in sums],
            *[pltpu.VMEM((2, *shape, H), F32) for shape in sums],
            pltpu.VMEM((2, NB, half_b, H), F32),
            pltpu.VMEM((2, NB, NZ - 1, half_b // NZ, H), F32),
            pltpu.SemaphoreType.DMA((points // STEP,)),
            pltpu.SemaphoreType.DMA,
            pltpu.SemaphoreType.DMA((5, 4)),
            pltpu.SemaphoreType.DMA((5, N)),
            pltpu.SemaphoreType.DMA((2, 5, N)),
            pltpu.SemaphoreType.DMA((2, 4, NB)),
            pltpu.SemaphoreType.DMA((2, 5, N)),
            pltpu.SemaphoreType.DMA((5, N)),
        ],
        compiler_params=pltpu.CompilerParams(
            collective_id=0, has_side_effects=True, vmem_limit_bytes=46 << 20
        ),
        cost_estimate=pl.CostEstimate(
            flops=18 * points * times * k, bytes_accessed=4 * points * times, transcendentals=0
        ),
    )(snapshots, sketch)
    hbm = pl.BlockSpec(memory_space=pl.ANY)
    return pl.pallas_call(
        store,
        name="store",
        out_shape=[jax.ShapeDtypeStruct((points, k), F32), jax.ShapeDtypeStruct((times, k), F32)],
        in_specs=[vmem, vmem],
        out_specs=[hbm, hbm],
        scratch_shapes=[pltpu.SemaphoreType.DMA((PIECES + 1,))],
        compiler_params=pltpu.CompilerParams(has_side_effects=True, vmem_limit_bytes=4 << 20),
    )(refined, cosample)


def solution(mesh):
    return jax.shard_map(
        local,
        mesh=mesh,
        in_specs=(P("space", "tm"), P("tm", None)),
        out_specs=(P("space", None), P("tm", None)),
        check_vma=False,
    )
```
